256 devices in a mesh: group: 16 (over z_hi, y), section: 2 (over z_lo), tensor: 8 (over x, core).
Axes of the slice: x: 4, y: 4, z: 8 (z_hi: 4, z_lo: 2; z = z_hi * 2 + z_lo), core: 2. Of those that a mesh axis runs over, the one named last changes fastest.
Arguments:
- hidden: bfloat16 [2, 64, 4, 8192], P('section', 'group', None, 'tensor'), may hold values from -6 to 6
- base_kv: bfloat16 [16, 8192, 256], P(('section', 'tensor')), may hold values from -0.0625 to 0.0625
- delta_codes: bfloat16 [16, 8192, 256], P(None, ('group', 'section', 'tensor')), may hold values from -448 to 448
- delta_scales: bfloat16 [16, 8192, 2], P(None, ('group', 'section', 'tensor')), may hold values from 1.9907951e-05 to 0.00019931793
- queries: bfloat16 [2, 64, 4, 8192], P('section', 'group', None, 'tensor'), may hold values from -4 to 4
- key_cache: bfloat16 [2, 64, 8, 4096, 128], P('section', 'group', 'tensor'), may hold values from -400 to 400
- value_cache: bfloat16 [2, 64, 8, 4096, 128], P('section', 'group', 'tensor'), may hold values from -6 to 6
- lengths: int32 [64], P('group'), may hold values from 1024 to 4096, as said below
Outputs:
- new_entries: bfloat16 [2, 64, 4, 2048], P('section', 'group', None, 'tensor')
- attended: bfloat16 [2, 64, 4, 8192], P('section', 'group', None, 'tensor')
The draws below stay inside these ranges and needn't reach their ends.
Inputs may be any that keep to these rules, and one draw needn't show every extreme that they name: `lengths`: some row has exactly 4096 cached positions and some row exactly 1024.
All inputs are finite; a program needn't handle non-finite values.
Results may differ from the reference program's by a relative error of at most 0.005.
Values may be sent and summed in bfloat16 or wider, within the bound.
A program may use at most 128 MiB of HBM per device.

```python
import math
import jax
import jax.numpy as jnp
from jax import lax

D = 8192
HD = 128
QH = 64
KVH = 8
CTX = 4096
STEPS = 4
LAYERS = 2
ROWS = 64
MINLEN = 1024


def base_queries(key):
    return jnp.clip(jax.random.normal(key, (LAYERS, ROWS, STEPS, QH * HD), jnp.float32), -4.0, 4.0)


def draw_queries(key, part):
    return base_queries(key).astype(jnp.bfloat16)


def draw_key_cache(key, part):
    key = jax.random.fold_in(key, 7)
    cached = jnp.clip(jax.random.normal(key, (LAYERS, ROWS, KVH, CTX, HD), jnp.float32), -4.0, 4.0)
    return cached.astype(jnp.bfloat16)


def draw_lengths(key, part):
    key = jax.random.fold_in(key, 5)
    first_key, second_key, third_key = jax.random.split(key, 3)
    drawn = jax.random.randint(first_key, (ROWS,), MINLEN, CTX + 1)
    longest = jax.random.randint(second_key, (), 0, ROWS)
    shortest = (longest + 1 + jax.random.randint(third_key, (), 0, ROWS - 1)) % ROWS
    places = jnp.arange(ROWS)
    drawn = jnp.where(places == longest, CTX, drawn)
    drawn = jnp.where(places == shortest, MINLEN, drawn)
    return drawn.astype(jnp.int32)


def steps_of(own_key, shape, cuts, smallest, largest):
    loudness = 1.0
    for axis_at, blocks in cuts:
        heights = jax.random.uniform(jax.random.fold_in(jax.random.fold_in(own_key, 6), axis_at), (blocks,), jnp.float32, smallest / len(cuts), largest / len(cuts))
        loudness = loudness * jnp.repeat(jnp.exp(heights), shape[axis_at] // blocks).reshape((-1,) + (1,) * (len(shape) - 1 - axis_at))
    return loudness


def normal_values(stream_key, shape, scale, reach, cuts=(), kind=jnp.bfloat16):
    result = scale * jax.random.normal(stream_key, shape, jnp.float32)
    if cuts:
        result = result * steps_of(stream_key, shape, cuts, -0.22, 0.18)
    return jnp.clip(result, -reach, reach).astype(kind)


def setup_inputs(seed: int = 0) -> dict:
    key_of = jax.random.split(jax.random.key(seed), 9)
    hidden = normal_values(key_of[0], (LAYERS, ROWS, STEPS, D), 1.0, 6.0, ((0, 2), (1, 16), (3, 8)))
    base_kv = normal_values(key_of[1], (LAYERS * KVH, D, 2 * HD), D ** -0.5, 0.0625, ((0, 16),))
    delta_codes = normal_values(key_of[2], (LAYERS * KVH, D, 2 * HD), 100.0, 448.0, ((1, 256),))
    delta_scales = jnp.clip(jnp.exp(math.log(0.00019931793) - 2.303782 * jax.random.uniform(key_of[3], (LAYERS * KVH, D, 2), jnp.float32) ** steps_of(key_of[3], (LAYERS * KVH, D, 2), ((1, 256),), -0.2, 0.2)), 1.990795135498047e-05, 0.00019931793).astype(jnp.bfloat16)
    queries = draw_queries(jax.random.fold_in(key_of[8], 71), 0)
    key_cache = draw_key_cache(jax.random.fold_in(key_of[8], 71), 0)
    value_cache = normal_values(key_of[6], (LAYERS, ROWS, KVH, CTX, HD), 1.0, 6.0, ((0, 2), (1, 16), (2, 8)))
    lengths = draw_lengths(jax.random.fold_in(key_of[8], 71), 0)
    return dict(hidden=hidden, base_kv=base_kv, delta_codes=delta_codes, delta_scales=delta_scales, queries=queries, key_cache=key_cache, value_cache=value_cache, lengths=lengths)


def rotate(key_part, positions):
    half_size = key_part.shape[-1] // 2
    freq_index = jnp.arange(half_size, dtype=jnp.float32)
    frequency = jnp.exp(freq_index * (-2.0 * math.log(1000000.0) / key_part.shape[-1]))
    phases = positions[..., None] * frequency
    cosine = jnp.cos(phases)
    sine_part = jnp.sin(phases)
    first_half = key_part[..., :half_size]
    second_half = key_part[..., half_size:]
    return jnp.concatenate([first_half * cosine - second_half * sine_part, second_half * cosine + first_half * sine_part], axis=-1)


def reference(hidden, base_kv, delta_codes, delta_scales, queries, key_cache, value_cache, lengths):
    group_size = QH // KVH
    scale_full = jnp.repeat(delta_scales.astype(jnp.float32), HD, axis=2)
    delta_weight = (delta_codes.astype(jnp.float32) * scale_full).astype(jnp.bfloat16)
    delta_weight = delta_weight.reshape(LAYERS, KVH, D, 2 * HD)
    base_blocks = base_kv.reshape(LAYERS, KVH, D, 2 * HD)
    offsets = jnp.arange(STEPS, dtype=jnp.int32)
    positions = (lengths[:, None] + offsets[None, :]).astype(jnp.float32)
    fresh_visible = (offsets[None, :] <= offsets[:, None])[None, :, None, :]
    score_scale = HD ** -0.5
    entry_list = []
    attended_list = []
    for layer_index in range(LAYERS):
        inputs = hidden[layer_index].astype(jnp.float32)
        projected = jnp.einsum("rtd,jdc->rtjc", inputs, base_blocks[layer_index].astype(jnp.float32))
        projected = projected + jnp.einsum("rtd,jdc->rtjc", inputs, delta_weight[layer_index].astype(jnp.float32))
        fresh_keys = rotate(projected[..., :HD], positions[:, :, None]).astype(jnp.bfloat16)
        fresh_values = projected[..., HD:].astype(jnp.bfloat16)
        entry_list.append(jnp.concatenate([fresh_keys, fresh_values], axis=-1).reshape(ROWS, STEPS, KVH * 2 * HD))

        def one_row(bundle):
            query_row, key_rows, value_rows, new_keys, new_values, length = bundle
            query_row = query_row.reshape(STEPS, KVH, group_size, HD).astype(jnp.float32)
            cache_scores = jnp.einsum("tjgh,jph->jtgp", query_row, key_rows.astype(jnp.float32)) * score_scale
            fresh_scores = jnp.einsum("tjgh,ujh->jtgu", query_row, new_keys.astype(jnp.float32)) * score_scale
            cache_visible = (jnp.arange(CTX, dtype=jnp.int32) < length)[None, None, None, :]
            peak_score = jnp.maximum(jnp.max(jnp.where(cache_visible, cache_scores, -jnp.inf), axis=-1), jnp.max(jnp.where(fresh_visible, fresh_scores, -jnp.inf), axis=-1))
            cache_exp = jnp.where(cache_visible, jnp.exp(cache_scores - peak_score[..., None]), 0.0)
            fresh_exp = jnp.where(fresh_visible, jnp.exp(fresh_scores - peak_score[..., None]), 0.0)
            normaliser = jnp.sum(cache_exp, axis=-1) + jnp.sum(fresh_exp, axis=-1)
            cache_weights = (cache_exp / normaliser[..., None]).astype(jnp.bfloat16)
            fresh_weights = (fresh_exp / normaliser[..., None]).astype(jnp.bfloat16)
            output = jnp.einsum("jtgp,jph->tjgh", cache_weights.astype(jnp.float32), value_rows.astype(jnp.float32))
            output = output + jnp.einsum("jtgu,ujh->tjgh", fresh_weights.astype(jnp.float32), new_values.astype(jnp.float32))
            return output.reshape(STEPS, QH * HD).astype(jnp.bfloat16)

        attended_list.append(lax.map(one_row, (queries[layer_index], key_cache[layer_index], value_cache[layer_index], fresh_keys, fresh_values, lengths)))
    return (jnp.stack(entry_list), jnp.stack(attended_list))
```

```python
import functools
import math

import jax
import jax.numpy as jnp
from jax import lax
from jax.experimental import pallas as pl
from jax.experimental.pallas import tpu as pltpu
from jax.sharding import PartitionSpec as P

MESH = pl.DeviceIdType.MESH
LOG2E = math.log2(math.e)
TURN = 4


def place(g, s, t):
    return {"group": g, "section": s, "tensor": t}


def kernel(
    hidden, base, codes, scales, queries, keys, values, lengths,
    entries, attended,
    hidden_v, queries_v, codes_v, scales_v, base_v, keys_v, values_v,
    delta_out, delta_in, half_out, hidden_in, part_out, part_in,
    score_v, best_v, norm_v, mix_v, entries_v, attended_v,
    load_sem, cache_sem, delta_send, delta_recv, half_send, half_recv, spread_send, spread_recv,
    part_send, part_recv, store_sem,
):
    groups, sections, tensors = 16, 2, 8
    blocks = sections * tensors
    g = lax.axis_index("group")
    s = lax.axis_index("section")
    t = lax.axis_index("tensor")
    me = s * tensors + t
    rows, steps = hidden_v.shape[0], hidden_v.shape[1]
    tokens = rows * steps
    owned = codes_v.shape[1]
    chunk = blocks * owned
    heads = queries_v.shape[2] // 128
    asks = heads * steps
    context = keys_v.shape[1]

    loads = [
        pltpu.make_async_copy(codes, codes_v, load_sem.at[0]),
        pltpu.make_async_copy(scales, scales_v, load_sem.at[1]),
        pltpu.make_async_copy(hidden.at[0], hidden_v, load_sem.at[2]),
        pltpu.make_async_copy(queries.at[0], queries_v, load_sem.at[3]),
        pltpu.make_async_copy(base.at[0, pl.ds(g * chunk, chunk), :], base_v, load_sem.at[4]),
    ]
    caches = []
    for r in range(rows):
        caches.append(
            (
                pltpu.make_async_copy(keys.at[0, r, 0], keys_v.at[r], cache_sem.at[0, r]),
                pltpu.make_async_copy(values.at[0, r, 0], values_v.at[r], cache_sem.at[1, r]),
            )
        )
    for load in loads[:4]:
        load.start()

    inside = []
    for j in range(1, blocks):
        other = lax.rem(me + j, blocks)
        inside.append((other, lax.div(other, tensors), lax.rem(other, tensors)))
    across = [lax.rem(g + j, groups) for j in range(1, groups)]
    pair = lax.rem(t + tensors - TURN, tensors)
    half_to = [(2 * t + h, lax.rem(lax.div(g, 2) + TURN, tensors)) for h in range(2)]
    half_from = [(2 * pair + h, lax.div(g, 2)) for h in range(2)]

    barrier = pltpu.get_barrier_semaphore()
    for _, os, ot in inside:
        pl.semaphore_signal(barrier, inc=1, device_id=place(g, os, ot), device_id_type=MESH)
    for og, ot in half_to + half_from:
        pl.semaphore_signal(barrier, inc=1, device_id=place(og, s, ot), device_id_type=MESH)
    for og in across:
        pl.semaphore_signal(barrier, inc=1, device_id=place(og, s, t), device_id_type=MESH)

    for r in range(rows):
        for load in caches[r]:
            load.start()
    loads[4].start()

    loads[2].wait()
    slab = jnp.concatenate([hidden_v[r].astype(jnp.float32) for r in range(rows)], axis=0)
    for h in range(2):
        half_out[h] = slab[:, h * chunk : (h + 1) * chunk].astype(jnp.bfloat16)

    loads[0].wait()
    loads[1].wait()
    flat = scales_v[...].astype(jnp.float32).reshape(blocks * 2, owned)
    turned = flat.T
    for b in range(blocks):
        code = codes_v[b].astype(jnp.float32)
        left = code[:, :128] * turned[:, 2 * b : 2 * b + 1]
        right = code[:, 128:] * turned[:, 2 * b + 1 : 2 * b + 2]
        delta_out[b] = jnp.concatenate([left, right], axis=1).astype(jnp.bfloat16)

    pl.semaphore_wait(barrier, len(inside) + len(half_to) + len(half_from) + len(across))

    half_copies = []
    for h in range(2):
        og, ot = half_to[h]
        half_copies.append(
            pltpu.make_async_remote_copy(
                src_ref=half_out.at[h],
                dst_ref=hidden_in.at[g],
                send_sem=half_send,
                recv_sem=half_recv,
                device_id=place(og, s, ot),
                device_id_type=MESH,
            )
        )
        half_copies[-1].start()
    for other, os, ot in inside:
        pltpu.make_async_remote_copy(
            src_ref=delta_out.at[other],
            dst_ref=delta_in.at[me],
            send_sem=delta_send,
            recv_sem=delta_recv,
            device_id=place(g, os, ot),
            device_id_type=MESH,
        ).start()
    pltpu.make_async_copy(delta_out.at[me], delta_in.at[me], delta_recv).start()

    loads[3].wait()
    asked = []
    for r in range(rows):
        block = queries_v[r].astype(jnp.float32)
        asked.append(
            jnp.concatenate([block[:, h * 128 : (h + 1) * 128] for h in range(heads)], axis=0).astype(jnp.bfloat16)
        )
    scale = 128 ** -0.5 * LOG2E

    def attend(r):
        caches[r][0].wait()
        score = lax.dot_general(
            asked[r], keys_v[r], (((1,), (1,)), ((), ())), preferred_element_type=jnp.float32
        ) * scale
        place_of = lax.broadcasted_iota(jnp.int32, (asks, context), 1)
        score = jnp.where(place_of < lengths[r], score, -jnp.inf)
        best = jnp.max(score, axis=1, keepdims=True)
        weight = jnp.exp2(score - best)
        norm = jnp.sum(weight, axis=1, keepdims=True)
        caches[r][1].wait()
        mix = jnp.dot(weight.astype(jnp.bfloat16), values_v[r], preferred_element_type=jnp.float32)
        best_v[pl.ds(r * asks, asks), :] = jnp.broadcast_to(best, (asks, 128))
        norm_v[pl.ds(r * asks, asks), :] = jnp.broadcast_to(norm, (asks, 128))
        mix_v[pl.ds(r * asks, asks), :] = mix

    attend(0)

    mine = hidden_in.at[pl.ds(2 * pair, 2)]
    pltpu.make_async_copy(mine, mine, half_recv).wait()
    for j in range(1, tensors):
        pltpu.make_async_remote_copy(
            src_ref=mine,
            dst_ref=mine,
            send_sem=spread_send,
            recv_sem=spread_recv,
            device_id=place(g, s, lax.rem(t + j, tensors)),
            device_id_type=MESH,
        ).start()

    attend(1)
    attend(2)
    attend(3)

    loads[4].wait()
    pltpu.make_async_copy(delta_in, delta_in, delta_recv).wait()
    most = hidden_in.at[pl.ds(0, 2 * (tensors - 1))]
    pltpu.make_async_copy(most, most, spread_recv).wait()
    features = hidden_in[...].reshape(groups * tokens, chunk)
    update = delta_in[...].reshape(chunk, 256)
    partial = jnp.dot(features, base_v[...], preferred_element_type=jnp.float32)
    partial = partial + jnp.dot(features, update, preferred_element_type=jnp.float32)
    part_out[...] = partial.reshape(groups, tokens, 256).astype(jnp.bfloat16)
    for og in across:
        pltpu.make_async_remote_copy(
            src_ref=part_out.at[og],
            dst_ref=part_in.at[g],
            send_sem=part_send,
            recv_sem=part_recv,
            device_id=place(og, s, t),
            device_id_type=MESH,
        ).start()
    pltpu.make_async_copy(part_out.at[g], part_in.at[g], part_recv).start()

    line = lax.broadcasted_iota(jnp.int32, (tokens, 128), 0)
    lane = lax.broadcasted_iota(jnp.int32, (tokens, 128), 1)
    start = jnp.zeros((tokens, 128), jnp.int32)
    for r in range(rows):
        start = jnp.where(line // steps == r, lengths[r], start)
    position = (start + line % steps).astype(jnp.float32)
    frequency = jnp.exp((lane % 64).astype(jnp.float32) * (-2.0 * math.log(1000000.0) / 128))
    phase = position * frequency
    cosine = jnp.cos(phase)
    sine = jnp.where(lane < 64, -jnp.sin(phase), jnp.sin(phase))

    pltpu.make_async_copy(part_in, part_in, part_recv).wait()
    projected = jnp.sum(part_in[...].astype(jnp.float32), axis=0)
    key = projected[:, :128]
    swapped = jnp.concatenate([key[:, 64:], key[:, :64]], axis=1)
    fresh_key = key * cosine + swapped * sine
    fresh_value = projected[:, 128:]
    for r in range(rows):
        lines = slice(r * steps, (r + 1) * steps)
        entries_v[r] = jnp.concatenate([fresh_key[lines], fresh_value[lines]], axis=1).astype(jnp.bfloat16)
    store_entries = pltpu.make_async_copy(entries_v, entries.at[0], store_sem.at[0])
    store_entries.start()

    every = jnp.concatenate(asked, axis=0)
    total = rows * asks
    score = lax.dot_general(
        every, fresh_key.astype(jnp.bfloat16), (((1,), (1,)), ((), ())), preferred_element_type=jnp.float32
    ) * scale
    line = lax.broadcasted_iota(jnp.int32, (total, tokens), 0)
    col = lax.broadcasted_iota(jnp.int32, (total, tokens), 1)
    seen = (line // asks == col // steps) & (col % steps <= line % steps)
    score = jnp.where(seen, score, -jnp.inf)
    best_old = best_v[:, :1]
    best = jnp.maximum(best_old, jnp.max(score, axis=1, keepdims=True))
    weight = jnp.exp2(score - best)
    decay = jnp.exp2(best_old - best)
    norm = norm_v[:, :1] * decay + jnp.sum(weight, axis=1, keepdims=True)
    mix = mix_v[...] * decay + jnp.dot(
        weight.astype(jnp.bfloat16), fresh_value.astype(jnp.bfloat16), preferred_element_type=jnp.float32
    )
    result = mix / norm
    for r in range(rows):
        for h in range(heads):
            at = r * asks + h * steps
            attended_v[r, :, h * 128 : (h + 1) * 128] = result[at : at + steps].astype(jnp.bfloat16)
    store_attended = pltpu.make_async_copy(attended_v, attended.at[0], store_sem.at[1])
    store_attended.start()

    for copy in half_copies:
        copy.wait_send()
    sent = delta_out.at[pl.ds(0, blocks - 1)]
    pltpu.make_async_copy(sent, sent, delta_send).wait()
    pltpu.make_async_copy(most, most, spread_send).wait()
    sent = part_out.at[pl.ds(0, groups - 1)]
    pltpu.make_async_copy(sent, sent, part_send).wait()
    store_entries.wait()
    store_attended.wait()


def body(hidden, base_kv, delta_codes, delta_scales, queries, key_cache, value_cache, lengths):
    rows, steps, slab = hidden.shape[1:]
    blocks, owned, width = delta_codes.shape
    chunk = blocks * owned
    context = key_cache.shape[3]
    groups = lax.axis_size("group")
    tokens = rows * steps
    asks = rows * queries.shape[3] // 128 * steps
    any_space = pl.BlockSpec(memory_space=pl.ANY)
    bf16, f32 = jnp.bfloat16, jnp.float32
    return pl.pallas_call(
        kernel,
        out_shape=(
            jax.ShapeDtypeStruct((1, rows, steps, width), bf16),
            jax.ShapeDtypeStruct((1, rows, steps, queries.shape[3]), bf16),
        ),
        in_specs=[any_space] * 7 + [pl.BlockSpec(memory_space=pltpu.SMEM)],
        out_specs=[any_space, any_space],
        scratch_shapes=[
            pltpu.VMEM((rows, steps, slab), bf16),
            pltpu.VMEM((rows, steps, queries.shape[3]), bf16),
            pltpu.VMEM((blocks, owned, width), bf16),
            pltpu.VMEM((blocks, 2, owned), bf16),
            pltpu.VMEM((chunk, width), bf16),
            pltpu.VMEM((rows, context, 128), bf16),
            pltpu.VMEM((rows, context, 128), bf16),
            pltpu.VMEM((blocks, owned, width), bf16),
            pltpu.VMEM((blocks, owned, width), bf16),
            pltpu.VMEM((2, tokens, chunk), bf16),
            pltpu.VMEM((groups, tokens, chunk), bf16),
            pltpu.VMEM((groups, tokens, width), bf16),
            pltpu.VMEM((groups, tokens, width), bf16),
            pltpu.VMEM((8, 128), f32),
            pltpu.VMEM((asks, 128), f32),
            pltpu.VMEM((asks, 128), f32),
            pltpu.VMEM((asks, 128), f32),
            pltpu.VMEM((rows, steps, width), bf16),
            pltpu.VMEM((rows, steps, queries.shape[3]), bf16),
            pltpu.SemaphoreType.DMA((5,)),
            pltpu.SemaphoreType.DMA((2, rows)),
            pltpu.SemaphoreType.DMA,
            pltpu.SemaphoreType.DMA,
            pltpu.SemaphoreType.DMA,
            pltpu.SemaphoreType.DMA,
            pltpu.SemaphoreType.DMA,
            pltpu.SemaphoreType.DMA,
            pltpu.SemaphoreType.DMA,
            pltpu.SemaphoreType.DMA,
            pltpu.SemaphoreType.DMA((2,)),
        ],
        compiler_params=pltpu.CompilerParams(
            collective_id=0, has_side_effects=True, vmem_limit_bytes=62 * 1024 * 1024
        ),
    )(
        hidden, base_kv, delta_codes, jnp.transpose(delta_scales, (0, 2, 1)),
        queries, key_cache, value_cache, lengths,
    )


def solution(mesh):
    placed = (
        P("section", "group", None, "tensor"),
        P(("section", "tensor"), None, None),
        P(None, ("group", "section", "tensor"), None),
        P(None, ("group", "section", "tensor"), None),
        P("section", "group", None, "tensor"),
        P("section", "group", "tensor", None, None),
        P("section", "group", "tensor", None, None),
        P("group"),
    )
    return jax.shard_map(
        body,
        mesh=mesh,
        in_specs=placed,
        out_specs=(P("section", "group", None, "tensor"), P("section", "group", None, "tensor")),
        check_vma=False,
    )
```

```python
import math

import jax
import jax.numpy as jnp
from jax import lax
from jax.experimental import pallas as pl
from jax.experimental.pallas import tpu as pltpu
from jax.sharding import PartitionSpec as P

MESH = pl.DeviceIdType.MESH
LOG2E = math.log2(math.e)
SCALE = 128 ** -0.5 * LOG2E
HIGH, WIDE, TENSORS, SECTIONS = 4, 4, 8, 2
GROUPS = HIGH * WIDE
BLOCKS = SECTIONS * TENSORS
HALF = GROUPS // 2


def exchange(
    hidden, base, codes, scales, queries, keys, values, lengths,
    projected, asked, best, norm, mix,
    hidden_v, queries_v, codes_v, scales_v, base_v, keys_v, values_v,
    delta_out, delta_in, half_out, hidden_in, part_out, part_in,
    load_sem, cache_sem, delta_send, delta_recv, pass_send, pass_recv, base_send, base_recv,
    half_send, half_recv, part_send, part_recv,
):
    g = lax.axis_index("group")
    s = lax.axis_index("section")
    t = lax.axis_index("tensor")
    me = s * TENSORS + t
    chip = lax.div(t, 2)
    core = lax.rem(t, 2)
    high = lax.div(g, WIDE)
    wide = lax.rem(g, WIDE)
    rows, steps = hidden_v.shape[0], hidden_v.shape[1]
    owned = codes_v.shape[1]
    chunk = BLOCKS * owned
    heads = queries_v.shape[2] // 128
    asks = heads * steps
    context = keys_v.shape[1]

    def at(og, os, ot):
        return {"group": og, "section": os, "tensor": ot}

    side = 1 - lax.div(wide, 2)
    first = 2 * (1 - core)
    sibling = 2 * chip + 1 - core
    inside = []
    for j in range(1, BLOCKS):
        other = lax.rem(me + j, BLOCKS)
        inside.append((other, at(g, lax.div(other, TENSORS), lax.rem(other, TENSORS))))
    turns = (2, 1, 3, 0)
    taken = []
    for i in turns:
        for j in range(2):
            oh = lax.rem(high + i, HIGH)
            taken.append((i, j, oh * 2 + j, oh * WIDE + first + j))

    barrier = pltpu.get_barrier_semaphore()
    for _, _, _, og in taken:
        pl.semaphore_signal(barrier, inc=1, device_id=at(og, s, lax.div(g, 2)), device_id_type=MESH)
    for j in range(1, GROUPS):
        og = lax.rem(g + j, GROUPS)
        pl.semaphore_signal(barrier, inc=1, device_id=at(og, s, 2 * chip + side), device_id_type=MESH)
    for _, there in inside:
        pl.semaphore_signal(barrier, inc=1, device_id=there, device_id_type=MESH)

    loads = [
        pltpu.make_async_copy(hidden.at[0], hidden_v, load_sem.at[0]),
        pltpu.make_async_copy(codes, codes_v, load_sem.at[1]),
        pltpu.make_async_copy(scales, scales_v, load_sem.at[2]),
        pltpu.make_async_copy(queries.at[0], queries_v, load_sem.at[3]),
        pltpu.make_async_copy(base.at[0, pl.ds(g * chunk, chunk), :], base_v.at[core], load_sem.at[4]),
    ]
    for load in loads:
        load.start()
    caches = []
    for r in range(rows):
        caches.append(
            (
                pltpu.make_async_copy(keys.at[0, r, 0], keys_v.at[r], cache_sem.at[0, r]),
                pltpu.make_async_copy(values.at[0, r, 0], values_v.at[r], cache_sem.at[1, r]),
            )
        )
        for load in caches[r]:
            load.start()

    loads[0].wait()
    slab = jnp.concatenate([hidden_v[r].astype(jnp.float32) for r in range(rows)], axis=0)
    for h in range(2):
        half_out[h] = slab[:, h * chunk : (h + 1) * chunk].astype(jnp.bfloat16)

    own = (side == core).astype(jnp.int32)
    pl.semaphore_wait(barrier, len(inside) + 2 * WIDE + 2 * HALF - 2 * own)

    half_copies = []
    for h in range(2):
        for i in turns:
            half_copies.append(
                pltpu.make_async_remote_copy(
                    src_ref=half_out.at[h],
                    dst_ref=hidden_in.at[high * 2 + lax.rem(wide, 2)],
                    send_sem=half_send,
                    recv_sem=half_recv,
                    device_id=at(2 * t + h, s, 2 * lax.rem(chip + i, 4) + side),
                    device_id_type=MESH,
                )
            )
            half_copies[-1].start()

    loads[1].wait()
    loads[2].wait()
    turned = scales_v[...].astype(jnp.float32).reshape(BLOCKS * 2, owned).T
    for b in range(BLOCKS):
        code = codes_v[b].astype(jnp.float32)
        left = code[:, :128] * turned[:, 2 * b : 2 * b + 1]
        right = code[:, 128:] * turned[:, 2 * b + 1 : 2 * b + 2]
        delta_out[b] = jnp.concatenate([left, right], axis=1).astype(jnp.bfloat16)
    for other, there in inside:
        pltpu.make_async_remote_copy(
            src_ref=delta_out.at[other],
            dst_ref=delta_in.at[lax.rem(other, 2), me],
            send_sem=delta_send,
            recv_sem=delta_recv,
            device_id=there,
            device_id_type=MESH,
        ).start()
    pltpu.make_async_copy(delta_out.at[me], delta_in.at[core, me], delta_recv).start()

    loads[4].wait()
    base_copy = pltpu.make_async_remote_copy(
        src_ref=base_v.at[core],
        dst_ref=base_v.at[core],
        send_sem=base_send,
        recv_sem=base_recv,
        device_id=at(g, s, sibling),
        device_id_type=MESH,
    )
    base_copy.start()

    loads[3].wait()
    for r in range(rows):
        block = queries_v[r].astype(jnp.float32)
        asked[pl.ds(r * asks, asks), :] = jnp.concatenate(
            [block[:, h * 128 : (h + 1) * 128] for h in range(heads)], axis=0
        ).astype(jnp.bfloat16)

    def attend(r):
        lines = pl.ds(r * asks, asks)
        caches[r][0].wait()
        score = lax.dot_general(
            asked[lines, :], keys_v[r], (((1,), (1,)), ((), ())), preferred_element_type=jnp.float32
        ) * SCALE
        place = lax.broadcasted_iota(jnp.int32, (asks, context), 1)
        score = jnp.where(place < lengths[r], score, -jnp.inf)
        peak = jnp.max(score, axis=1, keepdims=True)
        weight = jnp.exp2(score - peak)
        total = jnp.sum(weight, axis=1, keepdims=True)
        caches[r][1].wait()
        best[lines, :] = jnp.broadcast_to(peak, (asks, 128))
        norm[lines, :] = jnp.broadcast_to(total, (asks, 128))
        mix[lines, :] = jnp.dot(weight.astype(jnp.bfloat16), values_v[r], preferred_element_type=jnp.float32)

    attend(0)
    attend(1)

    mine = delta_in.at[core]
    pltpu.make_async_copy(mine, mine, delta_recv).wait()
    pass_copy = pltpu.make_async_remote_copy(
        src_ref=mine,
        dst_ref=mine,
        send_sem=pass_send,
        recv_sem=pass_recv,
        device_id=at(g, s, sibling),
        device_id_type=MESH,
    )
    pass_copy.start()

    attend(2)
    attend(3)

    base_copy.wait_recv()
    pass_copy.wait_recv()
    pltpu.make_async_copy(hidden_in, hidden_in, half_recv).wait()
    features = hidden_in[...].reshape(HALF * rows * steps, chunk)
    for c in range(2):
        part = jnp.dot(features, base_v[c], preferred_element_type=jnp.float32)
        part = part + jnp.dot(
            features, delta_in[c].reshape(chunk, part.shape[1]), preferred_element_type=jnp.float32
        )
        part_out[c] = part.reshape(HALF, rows * steps, part.shape[1]).astype(jnp.bfloat16)

    def send_part(c, slot, og):
        return pltpu.make_async_remote_copy(
            src_ref=part_out.at[c, slot],
            dst_ref=part_in.at[g],
            send_sem=part_send,
            recv_sem=part_recv,
            device_id=at(og, s, 2 * chip + c),
            device_id_type=MESH,
        )

    for i, j, slot, og in taken:
        for c in range(2):
            if i == 0:
                local = (og == g) & (core == c)

                @pl.when(local)
                def _():
                    pltpu.make_async_copy(part_out.at[c, slot], part_in.at[g], part_recv).start()

                @pl.when(jnp.logical_not(local))
                def _():
                    send_part(c, slot, og).start()
            else:
                send_part(c, slot, og).start()

    pltpu.make_async_copy(part_in, part_in, part_recv).wait()
    projected[...] = jnp.sum(part_in[...].astype(jnp.float32), axis=0)

    for copy in half_copies:
        copy.wait_send()
    sent = delta_out.at[pl.ds(0, BLOCKS - 1)]
    pltpu.make_async_copy(sent, sent, delta_send).wait()
    base_copy.wait_send()
    pass_copy.wait_send()
    for i, j, slot, og in taken:
        for c in range(2):
            if i == 0:

                @pl.when(jnp.logical_not((og == g) & (core == c)))
                def _():
                    send_part(c, slot, og).wait_send()
            else:
                send_part(c, slot, og).wait_send()


def finish(lengths, projected, asked, best, norm, mix, entries, attended, entries_v, attended_v, store_sem):
    rows, steps = entries_v.shape[0], entries_v.shape[1]
    tokens = rows * steps
    total = asked.shape[0]
    asks = total // rows
    heads = asks // steps

    line = lax.broadcasted_iota(jnp.int32, (tokens, 128), 0)
    lane = lax.broadcasted_iota(jnp.int32, (tokens, 128), 1)
    start = jnp.zeros((tokens, 128), jnp.int32)
    for r in range(rows):
        start = jnp.where(line // steps == r, lengths[r], start)
    position = (start + line % steps).astype(jnp.float32)
    frequency = jnp.exp((lane % 64).astype(jnp.float32) * (-2.0 * math.log(1000000.0) / 128))
    phase = position * frequency
    cosine = jnp.cos(phase)
    sine = jnp.where(lane < 64, -jnp.sin(phase), jnp.sin(phase))

    key = projected[:, :128]
    swapped = jnp.concatenate([key[:, 64:], key[:, :64]], axis=1)
    fresh_key = key * cosine + swapped * sine
    fresh_value = projected[:, 128:]
    for r in range(rows):
        lines = slice(r * steps, (r + 1) * steps)
        entries_v[r] = jnp.concatenate([fresh_key[lines], fresh_value[lines]], axis=1).astype(jnp.bfloat16)
    store_entries = pltpu.make_async_copy(entries_v, entries.at[0], store_sem.at[0])
    store_entries.start()

    score = lax.dot_general(
        asked[...], fresh_key.astype(jnp.bfloat16), (((1,), (1,)), ((), ())), preferred_element_type=jnp.float32
    ) * SCALE
    line = lax.broadcasted_iota(jnp.int32, (total, tokens), 0)
    col = lax.broadcasted_iota(jnp.int32, (total, tokens), 1)
    seen = (line // asks == col // steps) & (col % steps <= line % steps)
    score = jnp.where(seen, score, -jnp.inf)
    old = best[:, :1]
    peak = jnp.maximum(old, jnp.max(score, axis=1, keepdims=True))
    weight = jnp.exp2(score - peak)
    decay = jnp.exp2(old - peak)
    whole = norm[:, :1] * decay + jnp.sum(weight, axis=1, keepdims=True)
    result = mix[...] * decay + jnp.dot(
        weight.astype(jnp.bfloat16), fresh_value.astype(jnp.bfloat16), preferred_element_type=jnp.float32
    )
    result = result / whole
    for r in range(rows):
        for h in range(heads):
            at = r * asks + h * steps
            attended_v[r, :, h * 128 : (h + 1) * 128] = result[at : at + steps].astype(jnp.bfloat16)
    store_attended = pltpu.make_async_copy(attended_v, attended.at[0], store_sem.at[1])
    store_attended.start()
    store_entries.wait()
    store_attended.wait()


def body(hidden, base_kv, delta_codes, delta_scales, queries, key_cache, value_cache, lengths):
    rows, steps, slab = hidden.shape[1:]
    owned, width = delta_codes.shape[1:]
    chunk = BLOCKS * owned
    context = key_cache.shape[3]
    query_width = queries.shape[3]
    tokens = rows * steps
    asks = rows * query_width // 128 * steps
    anywhere = pl.BlockSpec(memory_space=pl.ANY)
    scalars = pl.BlockSpec(memory_space=pltpu.SMEM)
    fast = pl.BlockSpec(memory_space=pltpu.VMEM)
    bf16, f32 = jnp.bfloat16, jnp.float32
    dma = pltpu.SemaphoreType.DMA
    middle = pl.pallas_call(
        exchange,
        out_shape=(
            pltpu.VMEM((tokens, width), f32),
            pltpu.VMEM((asks, 128), bf16),
            pltpu.VMEM((asks, 128), f32),
            pltpu.VMEM((asks, 128), f32),
            pltpu.VMEM((asks, 128), f32),
        ),
        in_specs=[anywhere] * 7 + [scalars],
        out_specs=[fast] * 5,
        scratch_shapes=[
            pltpu.VMEM((rows, steps, slab), bf16),
            pltpu.VMEM((rows, steps, query_width), bf16),
            pltpu.VMEM((BLOCKS, owned, width), bf16),
            pltpu.VMEM((BLOCKS, 2, owned), bf16),
            pltpu.VMEM((2, chunk, width), bf16),
            pltpu.VMEM((rows, context, 128), bf16),
            pltpu.VMEM((rows, context, 128), bf16),
            pltpu.VMEM((BLOCKS, owned, width), bf16),
            pltpu.VMEM((2, BLOCKS, owned, width), bf16),
            pltpu.VMEM((2, tokens, chunk), bf16),
            pltpu.VMEM((HALF, tokens, chunk), bf16),
            pltpu.VMEM((2, HALF, tokens, width), bf16),
            pltpu.VMEM((GROUPS, tokens, width), bf16),
            dma((5,)),
            dma((2, rows)),
            dma, dma, dma, dma, dma, dma, dma, dma, dma, dma,
        ],
        compiler_params=pltpu.CompilerParams(
            collective_id=0, has_side_effects=True, vmem_limit_bytes=60 * 1024 * 1024
        ),
    )(
        hidden, base_kv, delta_codes, jnp.transpose(delta_scales, (0, 2, 1)),
        queries, key_cache, value_cache, lengths,
    )
    return pl.pallas_call(
        finish,
        out_shape=(
            jax.ShapeDtypeStruct((1, rows, steps, width), bf16),
            jax.ShapeDtypeStruct((1, rows, steps, query_width), bf16),
        ),
        in_specs=[scalars] + [fast] * 5,
        out_specs=[anywhere, anywhere],
        scratch_shapes=[
            pltpu.VMEM((rows, steps, width), bf16),
            pltpu.VMEM((rows, steps, query_width), bf16),
            dma((2,)),
        ],
        compiler_params=pltpu.CompilerParams(vmem_limit_bytes=8 * 1024 * 1024),
    )(lengths, *middle)


def solution(mesh):
    placed = (
        P("section", "group", None, "tensor"),
        P(("section", "tensor"), None, None),
        P(None, ("group", "section", "tensor"), None),
        P(None, ("group", "section", "tensor"), None),
        P("section", "group", None, "tensor"),
        P("section", "group", "tensor", None, None),
        P("section", "group", "tensor", None, None),
        P("group"),
    )
    return jax.shard_map(
        body,
        mesh=mesh,
        in_specs=placed,
        out_specs=(P("section", "group", None, "tensor"), P("section", "group", None, "tensor")),
        check_vma=False,
    )
```

```python
import math

import jax
import jax.numpy as jnp
from jax import lax
from jax.experimental import pallas as pl
from jax.experimental.pallas import tpu as pltpu
from jax.sharding import PartitionSpec as P

MESH = pl.DeviceIdType.MESH
LOG2E = math.log2(math.e)
SCALE = 128 ** -0.5 * LOG2E
HIGH, WIDE, TENSORS, SECTIONS = 4, 4, 8, 2
GROUPS = HIGH * WIDE
BLOCKS = SECTIONS * TENSORS
HALF = GROUPS // 2


def exchange(
    hidden, base, codes, scales, queries, keys, values, lengths,
    projected, asked, best, norm, mix,
    hidden_v, queries_v, codes_v, scales_v, base_v, keys_v, values_v,
    delta_out, delta_in, half_out, hidden_in, part_out, part_in,
    load_sem, cache_sem, delta_send, delta_recv, pass_send, pass_recv, base_send, base_recv,
    half_send, half_recv, spread_send, spread_recv, part_send, part_recv,
):
    g = lax.axis_index("group")
    s = lax.axis_index("section")
    t = lax.axis_index("tensor")
    me = s * TENSORS + t
    chip = lax.div(t, 2)
    core = lax.rem(t, 2)
    high = lax.div(g, WIDE)
    wide = lax.rem(g, WIDE)
    rows, steps = hidden_v.shape[0], hidden_v.shape[1]
    owned = codes_v.shape[1]
    chunk = BLOCKS * owned
    heads = queries_v.shape[2] // 128
    asks = heads * steps
    context = keys_v.shape[1]

    def at(og, os, ot):
        return {"group": og, "section": os, "tensor": ot}

    first = 2 * core
    sibling = 2 * chip + 1 - core
    turns = (2, 1, 3, 0)
    inside = []
    for i in turns:
        for ds in (1, 0):
            for dc in (1, 0):
                if i or ds or dc:
                    os, ot = lax.rem(s + ds, 2), 2 * lax.rem(chip + i, 4) + lax.rem(core + dc, 2)
                    inside.append((os * TENSORS + ot, at(g, os, ot)))
    relay = lax.rem(t + TENSORS // 2, TENSORS)
    relay_slot = 2 * lax.div(relay, 2)
    taken = []
    for i in turns:
        for j in (1, 0):
            oh = lax.rem(high + i, HIGH)
            taken.append((i, j, oh * 2 + j, oh * WIDE + first + j))

    barrier = pltpu.get_barrier_semaphore()
    for h in range(2):
        pl.semaphore_signal(barrier, inc=1, device_id=at(2 * relay + h, s, lax.div(g, 2)), device_id_type=MESH)
    for _, there in inside:
        pl.semaphore_signal(barrier, inc=1, device_id=there, device_id_type=MESH)

    loads = [
        pltpu.make_async_copy(hidden.at[0], hidden_v, load_sem.at[0]),
        pltpu.make_async_copy(codes, codes_v, load_sem.at[1]),
        pltpu.make_async_copy(scales, scales_v, load_sem.at[2]),
        pltpu.make_async_copy(queries.at[0], queries_v, load_sem.at[3]),
        pltpu.make_async_copy(base.at[0, pl.ds(g * chunk, chunk), :], base_v.at[core], load_sem.at[4]),
    ]
    for load in loads:
        load.start()
    caches = []
    for r in range(rows):
        caches.append(
            (
                pltpu.make_async_copy(keys.at[0, r, 0], keys_v.at[r], cache_sem.at[0, r]),
                pltpu.make_async_copy(values.at[0, r, 0], values_v.at[r], cache_sem.at[1, r]),
            )
        )
        for load in caches[r]:
            load.start()

    loads[0].wait()
    slab = jnp.concatenate([hidden_v[r].astype(jnp.float32) for r in range(rows)], axis=0)
    for h in range(2):
        half_out[h] = slab[:, h * chunk : (h + 1) * chunk].astype(jnp.bfloat16)

    loads[1].wait()
    loads[2].wait()
    turned = scales_v[...].astype(jnp.float32).reshape(BLOCKS * 2, owned).T
    for b in range(BLOCKS):
        code = codes_v[b].astype(jnp.float32)
        left = code[:, :128] * turned[:, 2 * b : 2 * b + 1]
        right = code[:, 128:] * turned[:, 2 * b + 1 : 2 * b + 2]
        delta_out[b] = jnp.concatenate([left, right], axis=1).astype(jnp.bfloat16)

    pl.semaphore_wait(barrier, len(inside) + 2)

    half_copies = []
    for h in range(2):
        half_copies.append(
            pltpu.make_async_remote_copy(
                src_ref=half_out.at[h],
                dst_ref=hidden_in.at[high * 2 + lax.rem(wide, 2)],
                send_sem=half_send,
                recv_sem=half_recv,
                device_id=at(2 * t + h, s, lax.rem(lax.div(g, 2) + TENSORS // 2, TENSORS)),
                device_id_type=MESH,
            )
        )
        half_copies[-1].start()
    for other, there in inside:
        pltpu.make_async_remote_copy(
            src_ref=delta_out.at[other],
            dst_ref=delta_in.at[lax.rem(other, 2), me],
            send_sem=delta_send,
            recv_sem=delta_recv,
            device_id=there,
            device_id_type=MESH,
        ).start()
    pltpu.make_async_copy(delta_out.at[me], delta_in.at[core, me], delta_recv).start()

    loads[4].wait()
    base_copy = pltpu.make_async_remote_copy(
        src_ref=base_v.at[core],
        dst_ref=base_v.at[core],
        send_sem=base_send,
        recv_sem=base_recv,
        device_id=at(g, s, sibling),
        device_id_type=MESH,
    )
    base_copy.start()

    loads[3].wait()
    for r in range(rows):
        block = queries_v[r].astype(jnp.float32)
        asked[pl.ds(r * asks, asks), :] = jnp.concatenate(
            [block[:, h * 128 : (h + 1) * 128] for h in range(heads)], axis=0
        ).astype(jnp.bfloat16)

    def attend(r):
        lines = pl.ds(r * asks, asks)
        caches[r][0].wait()
        score = lax.dot_general(
            asked[lines, :], keys_v[r], (((1,), (1,)), ((), ())), preferred_element_type=jnp.float32
        ) * SCALE
        place = lax.broadcasted_iota(jnp.int32, (asks, context), 1)
        score = jnp.where(place < lengths[r], score, -jnp.inf)
        peak = jnp.max(score, axis=1, keepdims=True)
        weight = jnp.exp2(score - peak)
        total = jnp.sum(weight, axis=1, keepdims=True)
        caches[r][1].wait()
        best[lines, :] = jnp.broadcast_to(peak, (asks, 128))
        norm[lines, :] = jnp.broadcast_to(total, (asks, 128))
        mix[lines, :] = jnp.dot(weight.astype(jnp.bfloat16), values_v[r], preferred_element_type=jnp.float32)

    attend(0)
    attend(1)

    here = hidden_in.at[pl.ds(relay_slot, 2)]
    pltpu.make_async_copy(here, here, half_recv).wait()
    spread_copies = []
    for i in turns[:3]:
        spread_copies.append(
            pltpu.make_async_remote_copy(
                src_ref=here,
                dst_ref=here,
                send_sem=spread_send,
                recv_sem=spread_recv,
                device_id=at(g, s, 2 * lax.rem(chip + i, 4) + core),
                device_id_type=MESH,
            )
        )
        spread_copies[-1].start()

    mine = delta_in.at[core]
    pltpu.make_async_copy(mine, mine, delta_recv).wait()
    pass_copy = pltpu.make_async_remote_copy(
        src_ref=mine,
        dst_ref=mine,
        send_sem=pass_send,
        recv_sem=pass_recv,
        device_id=at(g, s, sibling),
        device_id_type=MESH,
    )
    pass_copy.start()

    attend(2)
    attend(3)

    base_copy.wait_recv()
    pass_copy.wait_recv()
    most = hidden_in.at[pl.ds(0, HALF - 2)]
    pltpu.make_async_copy(most, most, spread_recv).wait()
    features = hidden_in[...].reshape(HALF * rows * steps, chunk)
    for c in range(2):
        part = jnp.dot(features, base_v[c], preferred_element_type=jnp.float32)
        part = part + jnp.dot(
            features, delta_in[c].reshape(chunk, part.shape[1]), preferred_element_type=jnp.float32
        )
        part_out[c] = part.reshape(HALF, rows * steps, part.shape[1]).astype(jnp.bfloat16)

    def send_part(c, slot, og):
        return pltpu.make_async_remote_copy(
            src_ref=part_out.at[c, slot],
            dst_ref=part_in.at[g],
            send_sem=part_send,
            recv_sem=part_recv,
            device_id=at(og, s, 2 * chip + c),
            device_id_type=MESH,
        )

    for i, j, slot, og in taken:
        for c in range(2):
            if i == 0:
                local = (og == g) & (core == c)

                @pl.when(local)
                def _():
                    pltpu.make_async_copy(part_out.at[c, slot], part_in.at[g], part_recv).start()

                @pl.when(jnp.logical_not(local))
                def _():
                    send_part(c, slot, og).start()
            else:
                send_part(c, slot, og).start()

    pltpu.make_async_copy(part_in, part_in, part_recv).wait()
    projected[...] = jnp.sum(part_in[...].astype(jnp.float32), axis=0)

    for copy in half_copies + spread_copies:
        copy.wait_send()
    sent = delta_out.at[pl.ds(0, BLOCKS - 1)]
    pltpu.make_async_copy(sent, sent, delta_send).wait()
    base_copy.wait_send()
    pass_copy.wait_send()
    for i, j, slot, og in taken:
        for c in range(2):
            if i == 0:

                @pl.when(jnp.logical_not((og == g) & (core == c)))
                def _():
                    send_part(c, slot, og).wait_send()
            else:
                send_part(c, slot, og).wait_send()


def finish(lengths, projected, asked, best, norm, mix, entries, attended, entries_v, attended_v, store_sem):
    rows, steps = entries_v.shape[0], entries_v.shape[1]
    tokens = rows * steps
    total = asked.shape[0]
    asks = total // rows
    heads = asks // steps

    line = lax.broadcasted_iota(jnp.int32, (tokens, 128), 0)
    lane = lax.broadcasted_iota(jnp.int32, (tokens, 128), 1)
    start = jnp.zeros((tokens, 128), jnp.int32)
    for r in range(rows):
        start = jnp.where(line // steps == r, lengths[r], start)
    position = (start + line % steps).astype(jnp.float32)
    frequency = jnp.exp((lane % 64).astype(jnp.float32) * (-2.0 * math.log(1000000.0) / 128))
    phase = position * frequency
    cosine = jnp.cos(phase)
    sine = jnp.where(lane < 64, -jnp.sin(phase), jnp.sin(phase))

    key = projected[:, :128]
    swapped = jnp.concatenate([key[:, 64:], key[:, :64]], axis=1)
    fresh_key = key * cosine + swapped * sine
    fresh_value = projected[:, 128:]
    for r in range(rows):
        lines = slice(r * steps, (r + 1) * steps)
        entries_v[r] = jnp.concatenate([fresh_key[lines], fresh_value[lines]], axis=1).astype(jnp.bfloat16)
    store_entries = pltpu.make_async_copy(entries_v, entries.at[0], store_sem.at[0])
    store_entries.start()

    score = lax.dot_general(
        asked[...], fresh_key.astype(jnp.bfloat16), (((1,), (1,)), ((), ())), preferred_element_type=jnp.float32
    ) * SCALE
    line = lax.broadcasted_iota(jnp.int32, (total, tokens), 0)
    col = lax.broadcasted_iota(jnp.int32, (total, tokens), 1)
    seen = (line // asks == col // steps) & (col % steps <= line % steps)
    score = jnp.where(seen, score, -jnp.inf)
    old = best[:, :1]
    peak = jnp.maximum(old, jnp.max(score, axis=1, keepdims=True))
    weight = jnp.exp2(score - peak)
    decay = jnp.exp2(old - peak)
    whole = norm[:, :1] * decay + jnp.sum(weight, axis=1, keepdims=True)
    result = mix[...] * decay + jnp.dot(
        weight.astype(jnp.bfloat16), fresh_value.astype(jnp.bfloat16), preferred_element_type=jnp.float32
    )
    result = result / whole
    for r in range(rows):
        for h in range(heads):
            at = r * asks + h * steps
            attended_v[r, :, h * 128 : (h + 1) * 128] = result[at : at + steps].astype(jnp.bfloat16)
    store_attended = pltpu.make_async_copy(attended_v, attended.at[0], store_sem.at[1])
    store_attended.start()
    store_entries.wait()
    store_attended.wait()


def body(hidden, base_kv, delta_codes, delta_scales, queries, key_cache, value_cache, lengths):
    rows, steps, slab = hidden.shape[1:]
    owned, width = delta_codes.shape[1:]
    chunk = BLOCKS * owned
    context = key_cache.shape[3]
    query_width = queries.shape[3]
    tokens = rows * steps
    asks = rows * query_width // 128 * steps
    anywhere = pl.BlockSpec(memory_space=pl.ANY)
    scalars = pl.BlockSpec(memory_space=pltpu.SMEM)
    fast = pl.BlockSpec(memory_space=pltpu.VMEM)
    bf16, f32 = jnp.bfloat16, jnp.float32
    dma = pltpu.SemaphoreType.DMA
    middle = pl.pallas_call(
        exchange,
        out_shape=(
            pltpu.VMEM((tokens, width), f32),
            pltpu.VMEM((asks, 128), bf16),
            pltpu.VMEM((asks, 128), f32),
            pltpu.VMEM((asks, 128), f32),
            pltpu.VMEM((asks, 128), f32),
        ),
        in_specs=[anywhere] * 7 + [scalars],
        out_specs=[fast] * 5,
        scratch_shapes=[
            pltpu.VMEM((rows, steps, slab), bf16),
            pltpu.VMEM((rows, steps, query_width), bf16),
            pltpu.VMEM((BLOCKS, owned, width), bf16),
            pltpu.VMEM((BLOCKS, 2, owned), bf16),
            pltpu.VMEM((2, chunk, width), bf16),
            pltpu.VMEM((rows, context, 128), bf16),
            pltpu.VMEM((rows, context, 128), bf16),
            pltpu.VMEM((BLOCKS, owned, width), bf16),
            pltpu.VMEM((2, BLOCKS, owned, width), bf16),
            pltpu.VMEM((2, tokens, chunk), bf16),
            pltpu.VMEM((HALF, tokens, chunk), bf16),
            pltpu.VMEM((2, HALF, tokens, width), bf16),
            pltpu.VMEM((GROUPS, tokens, width), bf16),
            dma((5,)),
            dma((2, rows)),
            dma, dma, dma, dma, dma, dma, dma, dma, dma, dma, dma, dma,
        ],
        compiler_params=pltpu.CompilerParams(
            collective_id=0, has_side_effects=True, vmem_limit_bytes=60 * 1024 * 1024
        ),
    )(
        hidden, base_kv, delta_codes, jnp.transpose(delta_scales, (0, 2, 1)),
        queries, key_cache, value_cache, lengths,
    )
    return pl.pallas_call(
        finish,
        out_shape=(
            jax.ShapeDtypeStruct((1, rows, steps, width), bf16),
            jax.ShapeDtypeStruct((1, rows, steps, query_width), bf16),
        ),
        in_specs=[scalars] + [fast] * 5,
        out_specs=[anywhere, anywhere],
        scratch_shapes=[
            pltpu.VMEM((rows, steps, width), bf16),
            pltpu.VMEM((rows, steps, query_width), bf16),
            dma((2,)),
        ],
        compiler_params=pltpu.CompilerParams(vmem_limit_bytes=8 * 1024 * 1024),
    )(lengths, *middle)


def solution(mesh):
    placed = (
        P("section", "group", None, "tensor"),
        P(("section", "tensor"), None, None),
        P(None, ("group", "section", "tensor"), None),
        P(None, ("group", "section", "tensor"), None),
        P("section", "group", None, "tensor"),
        P("section", "group", "tensor", None, None),
        P("section", "group", "tensor", None, None),
        P("group"),
    )
    return jax.shard_map(
        body,
        mesh=mesh,
        in_specs=placed,
        out_specs=(P("section", "group", None, "tensor"), P("section", "group", None, "tensor")),
        check_vma=False,
    )
```

```python
import math

import jax
import jax.numpy as jnp
from jax import lax
from jax.experimental import pallas as pl
from jax.experimental.pallas import tpu as pltpu
from jax.sharding import PartitionSpec as P

MESH = pl.DeviceIdType.MESH
LOG2E = math.log2(math.e)
SCALE = 128 ** -0.5 * LOG2E
HIGH, WIDE, TENSORS, SECTIONS = 4, 4, 8, 2
GROUPS = HIGH * WIDE
BLOCKS = SECTIONS * TENSORS
HALF = GROUPS // 2


def exchange(
    hidden, base, codes, scales, queries, keys, values, lengths,
    projected, asked, best, norm, mix,
    hidden_v, queries_v, codes_v, scales_v, base_v, keys_v, values_v,
    delta_out, delta_in, half_out, hidden_in, held, part_out, part_in,
    load_sem, cache_sem, delta_send, delta_recv, pass_send, pass_recv, base_send, base_recv,
    half_send, half_recv, held_recv, spread_send, spread_recv, part_send, part_recv, ready,
):
    g = lax.axis_index("group")
    s = lax.axis_index("section")
    t = lax.axis_index("tensor")
    me = s * TENSORS + t
    chip = lax.div(t, 2)
    core = lax.rem(t, 2)
    high = lax.div(g, WIDE)
    wide = lax.rem(g, WIDE)
    rows, steps = hidden_v.shape[0], hidden_v.shape[1]
    owned = codes_v.shape[1]
    chunk = BLOCKS * owned
    heads = queries_v.shape[2] // 128
    asks = heads * steps
    context = keys_v.shape[1]

    def at(og, os, ot):
        return {"group": og, "section": os, "tensor": ot}

    first = 2 * core
    sibling = 2 * chip + 1 - core
    turns = (2, 1, 3, 0)
    inside = []
    for i in turns:
        for ds in (1, 0):
            for dc in (1, 0):
                if i or ds or dc:
                    os, ot = lax.rem(s + ds, 2), 2 * lax.rem(chip + i, 4) + lax.rem(core + dc, 2)
                    inside.append((os * TENSORS + ot, at(g, os, ot)))
    early = high < 2
    mirror = WIDE * (HIGH - 1 - high) + wide
    relay = lax.rem(t + TENSORS // 2, TENSORS)
    relay_slot = 2 * lax.div(relay, 2)
    late_cores = [at(mirror, s, 2 * lax.rem(chip + i, 4) + core) for i in turns]
    barrier = pltpu.get_barrier_semaphore()

    @pl.when(early)
    def _():
        for h in range(2):
            for og in (mirror, g):
                pl.semaphore_signal(barrier, inc=1, device_id=at(2 * relay + h, s, lax.div(og, 2)), device_id_type=MESH)
        for there in late_cores:
            pl.semaphore_signal(barrier, inc=1, device_id=there, device_id_type=MESH)

    for _, there in inside:
        pl.semaphore_signal(barrier, inc=1, device_id=there, device_id_type=MESH)

    loads = [
        pltpu.make_async_copy(hidden.at[0], hidden_v, load_sem.at[0]),
        pltpu.make_async_copy(codes, codes_v, load_sem.at[1]),
        pltpu.make_async_copy(scales, scales_v, load_sem.at[2]),
        pltpu.make_async_copy(queries.at[0], queries_v, load_sem.at[3]),
        pltpu.make_async_copy(base.at[0, pl.ds(g * chunk, chunk), :], base_v.at[core], load_sem.at[4]),
    ]
    for load in loads:
        load.start()
    caches = []
    for r in range(rows):
        caches.append(
            (
                pltpu.make_async_copy(keys.at[0, r, 0], keys_v.at[r], cache_sem.at[0, r]),
                pltpu.make_async_copy(values.at[0, r, 0], values_v.at[r], cache_sem.at[1, r]),
            )
        )
        for load in caches[r]:
            load.start()

    loads[0].wait()
    slab = jnp.concatenate([hidden_v[r].astype(jnp.float32) for r in range(rows)], axis=0)
    for h in range(2):
        half_out[h] = slab[:, h * chunk : (h + 1) * chunk].astype(jnp.bfloat16)

    loads[1].wait()
    loads[2].wait()
    turned = scales_v[...].astype(jnp.float32).reshape(BLOCKS * 2, owned).T
    for b in range(BLOCKS):
        code = codes_v[b].astype(jnp.float32)
        left = code[:, :128] * turned[:, 2 * b : 2 * b + 1]
        right = code[:, 128:] * turned[:, 2 * b + 1 : 2 * b + 2]
        delta_out[b] = jnp.concatenate([left, right], axis=1).astype(jnp.bfloat16)

    pl.semaphore_wait(barrier, len(inside) + 2 + len(late_cores) * lax.div(high, 2))

    @pl.when(jnp.logical_not(early))
    def _():
        for there in late_cores:
            pl.semaphore_signal(ready, inc=1, device_id=there, device_id_type=MESH)

    def half_copy(h, target, sem):
        return pltpu.make_async_remote_copy(
            src_ref=half_out.at[h],
            dst_ref=target,
            send_sem=half_send,
            recv_sem=sem,
            device_id=at(
                WIDE * lax.div(chip * (HIGH - 1 - chip), 2) + 2 * core + h,
                s,
                lax.rem(lax.div(g, 2) + TENSORS // 2, TENSORS),
            ),
            device_id_type=MESH,
        )

    for_early = chip < 2
    place_here = lax.rem(wide, 2)

    @pl.when(for_early)
    def _():
        for h in range(2):
            half_copy(h, hidden_in.at[high * 2 + place_here], half_recv).start()

    @pl.when(jnp.logical_not(for_early))
    def _():
        for h in range(2):
            half_copy(h, held.at[place_here], held_recv).start()

    for other, there in inside:
        pltpu.make_async_remote_copy(
            src_ref=delta_out.at[other],
            dst_ref=delta_in.at[lax.rem(other, 2), me],
            send_sem=delta_send,
            recv_sem=delta_recv,
            device_id=there,
            device_id_type=MESH,
        ).start()
    pltpu.make_async_copy(delta_out.at[me], delta_in.at[core, me], delta_recv).start()

    loads[4].wait()
    base_copy = pltpu.make_async_remote_copy(
        src_ref=base_v.at[core],
        dst_ref=base_v.at[core],
        send_sem=base_send,
        recv_sem=base_recv,
        device_id=at(g, s, sibling),
        device_id_type=MESH,
    )
    base_copy.start()

    loads[3].wait()
    for r in range(rows):
        block = queries_v[r].astype(jnp.float32)
        asked[pl.ds(r * asks, asks), :] = jnp.concatenate(
            [block[:, h * 128 : (h + 1) * 128] for h in range(heads)], axis=0
        ).astype(jnp.bfloat16)

    def attend(r):
        lines = pl.ds(r * asks, asks)
        caches[r][0].wait()
        score = lax.dot_general(
            asked[lines, :], keys_v[r], (((1,), (1,)), ((), ())), preferred_element_type=jnp.float32
        ) * SCALE
        place = lax.broadcasted_iota(jnp.int32, (asks, context), 1)
        score = jnp.where(place < lengths[r], score, -jnp.inf)
        peak = jnp.max(score, axis=1, keepdims=True)
        weight = jnp.exp2(score - peak)
        total = jnp.sum(weight, axis=1, keepdims=True)
        caches[r][1].wait()
        best[lines, :] = jnp.broadcast_to(peak, (asks, 128))
        norm[lines, :] = jnp.broadcast_to(total, (asks, 128))
        mix[lines, :] = jnp.dot(weight.astype(jnp.bfloat16), values_v[r], preferred_element_type=jnp.float32)

    attend(0)
    attend(1)

    here = hidden_in.at[pl.ds(relay_slot, 2)]

    def spread_copy(i):
        return pltpu.make_async_remote_copy(
            src_ref=here,
            dst_ref=here,
            send_sem=spread_send,
            recv_sem=spread_recv.at[chip],
            device_id=at(g, s, 2 * lax.rem(chip + i, 4) + core),
            device_id_type=MESH,
        )

    def relay_copy(there):
        return pltpu.make_async_remote_copy(
            src_ref=held,
            dst_ref=here,
            send_sem=spread_send,
            recv_sem=spread_recv.at[chip],
            device_id=there,
            device_id_type=MESH,
        )

    @pl.when(early)
    def _():
        pltpu.make_async_copy(here, here, half_recv).wait()
        for i in turns[:3]:
            spread_copy(i).start()
        pl.semaphore_wait(ready, len(late_cores))
        pltpu.make_async_copy(held, held, held_recv).wait()
        for there in late_cores:
            relay_copy(there).start()

    mine = delta_in.at[core]
    pltpu.make_async_copy(mine, mine, delta_recv).wait()
    pass_copy = pltpu.make_async_remote_copy(
        src_ref=mine,
        dst_ref=mine,
        send_sem=pass_send,
        recv_sem=pass_recv,
        device_id=at(g, s, sibling),
        device_id_type=MESH,
    )
    pass_copy.start()

    attend(2)
    attend(3)

    base_copy.wait_recv()
    pass_copy.wait_recv()
    tokens = rows * steps
    part_size = HALF // 2

    def send_part(c, slot, og):
        return pltpu.make_async_remote_copy(
            src_ref=part_out.at[c, slot],
            dst_ref=part_in.at[g],
            send_sem=part_send,
            recv_sem=part_recv,
            device_id=at(og, s, 2 * chip + c),
            device_id_type=MESH,
        )

    sends = []
    for phase in range(2):
        for from_chip in (2 - 2 * phase, 3 - 2 * phase):

            @pl.when(jnp.logical_not(early & (chip == from_chip)))
            def _():
                pair = hidden_in.at[pl.ds(2 * ((from_chip + 2) % 4), 2)]
                pltpu.make_async_copy(pair, pair, spread_recv.at[from_chip]).wait()

        slots = pl.ds(phase * part_size, part_size)
        features = hidden_in[slots].reshape(part_size * tokens, chunk)
        for c in range(2):
            part = jnp.dot(features, base_v[c], preferred_element_type=jnp.float32)
            part = part + jnp.dot(
                features, delta_in[c].reshape(chunk, part.shape[1]), preferred_element_type=jnp.float32
            )
            part_out[c, slots] = part.reshape(part_size, tokens, part.shape[1]).astype(jnp.bfloat16)
        far = lax.rem(lax.div(high + 1, 2) + 1 - phase, 2)
        for near in range(2):
            oh = 2 * phase + (1 - far if near else far)
            for j in range(2):
                for c in range(2):
                    slot = 2 * oh + j
                    og = WIDE * oh + first + j
                    sends.append((c, slot, og, near))
                    if near:
                        local = (og == g) & (core == c)

                        @pl.when(local)
                        def _():
                            pltpu.make_async_copy(part_out.at[c, slot], part_in.at[g], part_recv).start()

                        @pl.when(jnp.logical_not(local))
                        def _():
                            send_part(c, slot, og).start()
                    else:
                        send_part(c, slot, og).start()

    pltpu.make_async_copy(part_in, part_in, part_recv).wait()
    projected[...] = jnp.sum(part_in[...].astype(jnp.float32), axis=0)

    for h in range(2):
        half_copy(h, held.at[place_here], held_recv).wait_send()

    @pl.when(early)
    def _():
        for i in turns[:3]:
            spread_copy(i).wait_send()
        for there in late_cores:
            relay_copy(there).wait_send()

    sent = delta_out.at[pl.ds(0, BLOCKS - 1)]
    pltpu.make_async_copy(sent, sent, delta_send).wait()
    base_copy.wait_send()
    pass_copy.wait_send()
    for c, slot, og, near in sends:
        if near:

            @pl.when(jnp.logical_not((og == g) & (core == c)))
            def _():
                send_part(c, slot, og).wait_send()
        else:
            send_part(c, slot, og).wait_send()


def finish(lengths, projected, asked, best, norm, mix, entries, attended, entries_v, attended_v, store_sem):
    rows, steps = entries_v.shape[0], entries_v.shape[1]
    tokens = rows * steps
    total = asked.shape[0]
    asks = total // rows
    heads = asks // steps

    line = lax.broadcasted_iota(jnp.int32, (tokens, 128), 0)
    lane = lax.broadcasted_iota(jnp.int32, (tokens, 128), 1)
    start = jnp.zeros((tokens, 128), jnp.int32)
    for r in range(rows):
        start = jnp.where(line // steps == r, lengths[r], start)
    position = (start + line % steps).astype(jnp.float32)
    frequency = jnp.exp((lane % 64).astype(jnp.float32) * (-2.0 * math.log(1000000.0) / 128))
    phase = position * frequency
    cosine = jnp.cos(phase)
    sine = jnp.where(lane < 64, -jnp.sin(phase), jnp.sin(phase))

    key = projected[:, :128]
    swapped = jnp.concatenate([key[:, 64:], key[:, :64]], axis=1)
    fresh_key = key * cosine + swapped * sine
    fresh_value = projected[:, 128:]
    for r in range(rows):
        lines = slice(r * steps, (r + 1) * steps)
        entries_v[r] = jnp.concatenate([fresh_key[lines], fresh_value[lines]], axis=1).astype(jnp.bfloat16)
    store_entries = pltpu.make_async_copy(entries_v, entries.at[0], store_sem.at[0])
    store_entries.start()

    score = lax.dot_general(
        asked[...], fresh_key.astype(jnp.bfloat16), (((1,), (1,)), ((), ())), preferred_element_type=jnp.float32
    ) * SCALE
    line = lax.broadcasted_iota(jnp.int32, (total, tokens), 0)
    col = lax.broadcasted_iota(jnp.int32, (total, tokens), 1)
    seen = (line // asks == col // steps) & (col % steps <= line % steps)
    score = jnp.where(seen, score, -jnp.inf)
    old = best[:, :1]
    peak = jnp.maximum(old, jnp.max(score, axis=1, keepdims=True))
    weight = jnp.exp2(score - peak)
    decay = jnp.exp2(old - peak)
    whole = norm[:, :1] * decay + jnp.sum(weight, axis=1, keepdims=True)
    result = mix[...] * decay + jnp.dot(
        weight.astype(jnp.bfloat16), fresh_value.astype(jnp.bfloat16), preferred_element_type=jnp.float32
    )
    result = result / whole
    for r in range(rows):
        for h in range(heads):
            at = r * asks + h * steps
            attended_v[r, :, h * 128 : (h + 1) * 128] = result[at : at + steps].astype(jnp.bfloat16)
    store_attended = pltpu.make_async_copy(attended_v, attended.at[0], store_sem.at[1])
    store_attended.start()
    store_entries.wait()
    store_attended.wait()


def body(hidden, base_kv, delta_codes, delta_scales, queries, key_cache, value_cache, lengths):
    rows, steps, slab = hidden.shape[1:]
    owned, width = delta_codes.shape[1:]
    chunk = BLOCKS * owned
    context = key_cache.shape[3]
    query_width = queries.shape[3]
    tokens = rows * steps
    asks = rows * query_width // 128 * steps
    anywhere = pl.BlockSpec(memory_space=pl.ANY)
    scalars = pl.BlockSpec(memory_space=pltpu.SMEM)
    fast = pl.BlockSpec(memory_space=pltpu.VMEM)
    bf16, f32 = jnp.bfloat16, jnp.float32
    dma = pltpu.SemaphoreType.DMA
    middle = pl.pallas_call(
        exchange,
        out_shape=(
            pltpu.VMEM((tokens, width), f32),
            pltpu.VMEM((asks, 128), bf16),
            pltpu.VMEM((asks, 128), f32),
            pltpu.VMEM((asks, 128), f32),
            pltpu.VMEM((asks, 128), f32),
        ),
        in_specs=[anywhere] * 7 + [scalars],
        out_specs=[fast] * 5,
        scratch_shapes=[
            pltpu.VMEM((rows, steps, slab), bf16),
            pltpu.VMEM((rows, steps, query_width), bf16),
            pltpu.VMEM((BLOCKS, owned, width), bf16),
            pltpu.VMEM((BLOCKS, 2, owned), bf16),
            pltpu.VMEM((2, chunk, width), bf16),
            pltpu.VMEM((rows, context, 128), bf16),
            pltpu.VMEM((rows, context, 128), bf16),
            pltpu.VMEM((BLOCKS, owned, width), bf16),
            pltpu.VMEM((2, BLOCKS, owned, width), bf16),
            pltpu.VMEM((2, tokens, chunk), bf16),
            pltpu.VMEM((HALF, tokens, chunk), bf16),
            pltpu.VMEM((2, tokens, chunk), bf16),
            pltpu.VMEM((2, HALF, tokens, width), bf16),
            pltpu.VMEM((GROUPS, tokens, width), bf16),
            dma((5,)),
            dma((2, rows)),
            dma, dma, dma, dma, dma, dma, dma, dma, dma, dma,
            dma((4,)), dma, dma, pltpu.SemaphoreType.REGULAR,
        ],
        compiler_params=pltpu.CompilerParams(
            collective_id=0, has_side_effects=True, vmem_limit_bytes=60 * 1024 * 1024
        ),
    )(
        hidden, base_kv, delta_codes, jnp.transpose(delta_scales, (0, 2, 1)),
        queries, key_cache, value_cache, lengths,
    )
    return pl.pallas_call(
        finish,
        out_shape=(
            jax.ShapeDtypeStruct((1, rows, steps, width), bf16),
            jax.ShapeDtypeStruct((1, rows, steps, query_width), bf16),
        ),
        in_specs=[scalars] + [fast] * 5,
        out_specs=[anywhere, anywhere],
        scratch_shapes=[
            pltpu.VMEM((rows, steps, width), bf16),
            pltpu.VMEM((rows, steps, query_width), bf16),
            dma((2,)),
        ],
        compiler_params=pltpu.CompilerParams(vmem_limit_bytes=8 * 1024 * 1024),
    )(lengths, *middle)


def solution(mesh):
    placed = (
        P("section", "group", None, "tensor"),
        P(("section", "tensor"), None, None),
        P(None, ("group", "section", "tensor"), None),
        P(None, ("group", "section", "tensor"), None),
        P("section", "group", None, "tensor"),
        P("section", "group", "tensor", None, None),
        P("section", "group", "tensor", None, None),
        P("group"),
    )
    return jax.shard_map(
        body,
        mesh=mesh,
        in_specs=placed,
        out_specs=(P("section", "group", None, "tensor"), P("section", "group", None, "tensor")),
        check_vma=False,
    )
```

```python
import math

import jax
import jax.numpy as jnp
from jax import lax
from jax.experimental import pallas as pl
from jax.experimental.pallas import tpu as pltpu
from jax.sharding import PartitionSpec as P

MESH = pl.DeviceIdType.MESH
LOG2E = math.log2(math.e)
SCALE = 128 ** -0.5 * LOG2E
HIGH, WIDE, TENSORS, SECTIONS = 4, 4, 8, 2
GROUPS = HIGH * WIDE
BLOCKS = SECTIONS * TENSORS
HALF = GROUPS // 2


def exchange(
    hidden, base, codes, scales, queries, keys, values, lengths,
    projected, asked, best, norm, mix, cosine, sine,
    hidden_v, queries_v, codes_v, scales_v, base_v, keys_v, values_v,
    delta_out, delta_in, half_out, hidden_in, held, part_out, part_in,
    load_sem, cache_sem, delta_send, delta_recv, pass_send, pass_recv, base_send, base_recv,
    half_send, half_recv, held_recv, spread_send, spread_recv, part_send, part_recv, ready,
):
    g = lax.axis_index("group")
    s = lax.axis_index("section")
    t = lax.axis_index("tensor")
    me = s * TENSORS + t
    chip = lax.div(t, 2)
    core = lax.rem(t, 2)
    high = lax.div(g, WIDE)
    wide = lax.rem(g, WIDE)
    rows, steps = hidden_v.shape[0], hidden_v.shape[1]
    owned = codes_v.shape[1]
    chunk = BLOCKS * owned
    heads = queries_v.shape[2] // 128
    asks = heads * steps
    context = keys_v.shape[1]

    def at(og, os, ot):
        return {"group": og, "section": os, "tensor": ot}

    first = 2 * core
    sibling = 2 * chip + 1 - core
    turns = (2, 1, 3, 0)
    inside = []
    for i in turns:
        for ds in (1, 0):
            for dc in (1, 0):
                if i or ds or dc:
                    os, ot = lax.rem(s + ds, 2), 2 * lax.rem(chip + i, 4) + lax.rem(core + dc, 2)
                    inside.append((os * TENSORS + ot, at(g, os, ot)))
    early = high < 2
    takes_late = chip < 2
    mirror = WIDE * (HIGH - 1 - high) + wide
    relay = lax.rem(t + TENSORS // 2, TENSORS)
    relay_slot = 2 * lax.div(relay, 2)
    early_high = 1 - lax.div(chip, 2)
    early_slot = 2 * early_high + lax.rem(chip, 2)
    late_cores = [at(mirror, s, 2 * lax.rem(chip + i, 4) + core) for i in turns]
    barrier = pltpu.get_barrier_semaphore()

    @pl.when(early)
    def _():
        source = WIDE * early_high + first + lax.rem(chip, 2)
        for og in (mirror, g):
            pl.semaphore_signal(barrier, inc=1, device_id=at(source, s, lax.div(og, 2)), device_id_type=MESH)
        for there in late_cores:
            pl.semaphore_signal(barrier, inc=1, device_id=there, device_id_type=MESH)

    @pl.when(takes_late)
    def _():
        for h in range(2):
            pl.semaphore_signal(barrier, inc=1, device_id=at(2 * relay + h, s, lax.div(g, 2)), device_id_type=MESH)

    for _, there in inside:
        pl.semaphore_signal(barrier, inc=1, device_id=there, device_id_type=MESH)

    loads = [
        pltpu.make_async_copy(hidden.at[0], hidden_v, load_sem.at[0]),
        pltpu.make_async_copy(codes, codes_v, load_sem.at[1]),
        pltpu.make_async_copy(scales, scales_v, load_sem.at[2]),
        pltpu.make_async_copy(queries.at[0], queries_v, load_sem.at[3]),
        pltpu.make_async_copy(base.at[0, pl.ds(g * chunk, chunk), :], base_v.at[core], load_sem.at[4]),
    ]
    for load in loads:
        load.start()
    caches = []
    for r in range(rows):
        caches.append(
            (
                pltpu.make_async_copy(keys.at[0, r, 0], keys_v.at[r], cache_sem.at[0, r]),
                pltpu.make_async_copy(values.at[0, r, 0], values_v.at[r], cache_sem.at[1, r]),
            )
        )
        for load in caches[r]:
            load.start()

    loads[0].wait()
    slab = jnp.concatenate([hidden_v[r].astype(jnp.float32) for r in range(rows)], axis=0)
    for h in range(2):
        half_out[h] = slab[:, h * chunk : (h + 1) * chunk].astype(jnp.bfloat16)

    loads[1].wait()
    loads[2].wait()
    turned = scales_v[...].astype(jnp.float32).reshape(BLOCKS * 2, owned).T
    for b in range(BLOCKS):
        code = codes_v[b].astype(jnp.float32)
        left = code[:, :128] * turned[:, 2 * b : 2 * b + 1]
        right = code[:, 128:] * turned[:, 2 * b + 1 : 2 * b + 2]
        delta_out[b] = jnp.concatenate([left, right], axis=1).astype(jnp.bfloat16)

    pl.semaphore_wait(barrier, len(inside) + 2 + len(late_cores) * lax.div(high, 2))

    @pl.when(jnp.logical_not(early))
    def _():
        for i in range(4):
            pl.semaphore_signal(ready, inc=1, device_id=at(mirror, s, 2 * i + core), device_id_type=MESH)

    place_here = lax.rem(wide, 2)
    place_there = hidden_in.at[high * 2 + place_here]
    is_early = 1 - lax.div(high, 2)
    relay_chip = is_early * (2 * (1 - high) + place_here) + (1 - is_early) * (high - 2)
    turn = 1 - is_early

    def half_copy(h, og, target, sem):
        return pltpu.make_async_remote_copy(
            src_ref=half_out.at[h],
            dst_ref=target,
            send_sem=half_send,
            recv_sem=sem,
            device_id=at(og, s, 2 * relay_chip + lax.div(wide, 2)),
            device_id_type=MESH,
        )

    relayed = early & (chip >= 2)
    via = is_early * lax.div(chip, 2)
    half_to = [WIDE * ((1 - via) * chip + via * (HIGH - 1 - chip)) + 2 * core + h for h in range(2)]
    stays = [(og == g) & (2 * relay_chip + lax.div(wide, 2) == t) for og in half_to]
    for h in range(2):
        for here_first, target, sem in (
            (jnp.logical_not(relayed), place_there, half_recv.at[turn]),
            (relayed, held, held_recv),
        ):

            @pl.when(here_first & stays[h])
            def _():
                pltpu.make_async_copy(half_out.at[h], target, sem).start()

            @pl.when(here_first & jnp.logical_not(stays[h]))
            def _():
                half_copy(h, half_to[h], target, sem).start()

    for other, there in inside:
        pltpu.make_async_remote_copy(
            src_ref=delta_out.at[other],
            dst_ref=delta_in.at[lax.rem(other, 2), me],
            send_sem=delta_send,
            recv_sem=delta_recv,
            device_id=there,
            device_id_type=MESH,
        ).start()
    pltpu.make_async_copy(delta_out.at[me], delta_in.at[core, me], delta_recv).start()

    loads[4].wait()
    base_copy = pltpu.make_async_remote_copy(
        src_ref=base_v.at[core],
        dst_ref=base_v.at[core],
        send_sem=base_send,
        recv_sem=base_recv,
        device_id=at(g, s, sibling),
        device_id_type=MESH,
    )
    base_copy.start()

    loads[3].wait()
    for r in range(rows):
        block = queries_v[r].astype(jnp.float32)
        asked[pl.ds(r * asks, asks), :] = jnp.concatenate(
            [block[:, h * 128 : (h + 1) * 128] for h in range(heads)], axis=0
        ).astype(jnp.bfloat16)

    def attend(r):
        lines = pl.ds(r * asks, asks)
        caches[r][0].wait()
        score = lax.dot_general(
            asked[lines, :], keys_v[r], (((1,), (1,)), ((), ())), preferred_element_type=jnp.float32
        ) * SCALE
        place = lax.broadcasted_iota(jnp.int32, (asks, context), 1)
        score = jnp.where(place < lengths[r], score, -jnp.inf)
        peak = jnp.max(score, axis=1, keepdims=True)
        weight = jnp.exp2(score - peak)
        total = jnp.sum(weight, axis=1, keepdims=True)
        caches[r][1].wait()
        best[lines, :] = jnp.broadcast_to(peak, (asks, 128))
        norm[lines, :] = jnp.broadcast_to(total, (asks, 128))
        mix[lines, :] = jnp.dot(weight.astype(jnp.bfloat16), values_v[r], preferred_element_type=jnp.float32)

    attend(0)
    attend(1)

    here = hidden_in.at[pl.ds(relay_slot, 2)]
    piece = hidden_in.at[early_slot]

    def spread_copy(ref, sem, i):
        return pltpu.make_async_remote_copy(
            src_ref=ref,
            dst_ref=ref,
            send_sem=spread_send,
            recv_sem=spread_recv.at[sem],
            device_id=at(g, s, 2 * lax.rem(chip + i, 4) + core),
            device_id_type=MESH,
        )

    def relay_copy(there):
        return pltpu.make_async_remote_copy(
            src_ref=held,
            dst_ref=piece,
            send_sem=spread_send,
            recv_sem=spread_recv.at[early_slot],
            device_id=there,
            device_id_type=MESH,
        )

    @pl.when(early)
    def _():
        pltpu.make_async_copy(piece, piece, half_recv.at[0]).wait()
        for i in turns[:3]:
            spread_copy(piece, early_slot, i).start()
        pl.semaphore_wait(ready, len(late_cores))
        pltpu.make_async_copy(held, held, held_recv).wait()
        for there in late_cores:
            relay_copy(there).start()

    attend(2)

    mine = delta_in.at[core]
    pltpu.make_async_copy(mine, mine, delta_recv).wait()
    pass_copy = pltpu.make_async_remote_copy(
        src_ref=mine,
        dst_ref=mine,
        send_sem=pass_send,
        recv_sem=pass_recv,
        device_id=at(g, s, sibling),
        device_id_type=MESH,
    )
    pass_copy.start()

    @pl.when(takes_late)
    def _():
        pltpu.make_async_copy(here, here, half_recv.at[1]).wait()
        for i in turns[:3]:
            spread_copy(here, 4 + chip, i).start()

    base_copy.wait_recv()
    pass_copy.wait_recv()
    tokens = rows * steps

    def send_part(c, slot, og):
        return pltpu.make_async_remote_copy(
            src_ref=part_out.at[c, slot],
            dst_ref=part_in.at[g],
            send_sem=part_send,
            recv_sem=part_recv,
            device_id=at(og, s, 2 * chip + c),
            device_id_type=MESH,
        )

    sends = []
    for highs in ((0,), (1,), (2, 3)):
        if highs[0] < 2:
            arrivals = [(j, 1, early & (chip == 2 * (1 - highs[0]) + j), 2 * highs[0] + j) for j in range(2)]
        else:
            arrivals = [(2 * (oh - highs[0]), 2, chip == oh - 2, 4 + oh - 2) for oh in highs]
        for offset, size, taken_here, sem in arrivals:

            @pl.when(jnp.logical_not(taken_here))
            def _():
                arrived = hidden_in.at[pl.ds(2 * highs[0] + offset, size)]
                pltpu.make_async_copy(arrived, arrived, spread_recv.at[sem]).wait()

        slots = pl.ds(2 * highs[0], 2 * len(highs))
        features = hidden_in[slots].reshape(2 * len(highs) * tokens, chunk)
        for c in (1, 0):
            part = jnp.dot(features, base_v[c], preferred_element_type=jnp.float32)
            part = part + jnp.dot(
                features, delta_in[c].reshape(chunk, part.shape[1]), preferred_element_type=jnp.float32
            )
            part_out[c, slots] = part.reshape(2 * len(highs), tokens, part.shape[1]).astype(jnp.bfloat16)
            for oh in highs:
                for j in range(2):
                    slot = 2 * oh + j
                    og = WIDE * oh + first + j
                    sends.append((c, slot, og))
                    local = (og == g) & (core == c)

                    @pl.when(local)
                    def _():
                        pltpu.make_async_copy(part_out.at[c, slot], part_in.at[g], part_recv).start()

                    @pl.when(jnp.logical_not(local))
                    def _():
                        send_part(c, slot, og).start()

    attend(3)

    line = lax.broadcasted_iota(jnp.int32, (tokens, 128), 0)
    lane = lax.broadcasted_iota(jnp.int32, (tokens, 128), 1)
    start = jnp.zeros((tokens, 128), jnp.int32)
    for r in range(rows):
        start = jnp.where(line // steps == r, lengths[r], start)
    position = (start + line % steps).astype(jnp.float32)
    frequency = jnp.exp((lane % 64).astype(jnp.float32) * (-2.0 * math.log(1000000.0) / 128))
    phase = position * frequency
    cosine[...] = jnp.cos(phase)
    turned_sine = jnp.sin(phase)
    sine[...] = jnp.where(lane < 64, -turned_sine, turned_sine)

    pltpu.make_async_copy(part_in, part_in, part_recv).wait()
    projected[...] = jnp.sum(part_in[...].astype(jnp.float32), axis=0)

    for h in range(2):

        @pl.when(jnp.logical_not(stays[h]))
        def _():
            half_copy(h, g, place_there, half_recv.at[0]).wait_send()

    @pl.when(takes_late)
    def _():
        for i in turns[:3]:
            spread_copy(here, 4 + chip, i).wait_send()

    @pl.when(early)
    def _():
        for i in turns[:3]:
            spread_copy(piece, early_slot, i).wait_send()
        for there in late_cores:
            relay_copy(there).wait_send()

    sent = delta_out.at[pl.ds(0, BLOCKS - 1)]
    pltpu.make_async_copy(sent, sent, delta_send).wait()
    base_copy.wait_send()
    pass_copy.wait_send()
    for c, slot, og in sends:

        @pl.when(jnp.logical_not((og == g) & (core == c)))
        def _():
            send_part(c, slot, og).wait_send()


def finish(projected, asked, best, norm, mix, cosine, sine, entries, attended, entries_v, attended_v, store_sem):
    rows, steps = entries_v.shape[0], entries_v.shape[1]
    tokens = rows * steps
    total = asked.shape[0]
    asks = total // rows
    heads = asks // steps

    key = projected[:, :128]
    swapped = jnp.concatenate([key[:, 64:], key[:, :64]], axis=1)
    fresh_key = key * cosine[...] + swapped * sine[...]
    fresh_value = projected[:, 128:]
    for r in range(rows):
        lines = slice(r * steps, (r + 1) * steps)
        entries_v[r] = jnp.concatenate([fresh_key[lines], fresh_value[lines]], axis=1).astype(jnp.bfloat16)
    store_entries = pltpu.make_async_copy(entries_v, entries.at[0], store_sem.at[0])
    store_entries.start()

    score = lax.dot_general(
        asked[...], fresh_key.astype(jnp.bfloat16), (((1,), (1,)), ((), ())), preferred_element_type=jnp.float32
    ) * SCALE
    line = lax.broadcasted_iota(jnp.int32, (total, tokens), 0)
    col = lax.broadcasted_iota(jnp.int32, (total, tokens), 1)
    seen = (line // asks == col // steps) & (col % steps <= line % steps)
    score = jnp.where(seen, score, -jnp.inf)
    old = best[:, :1]
    peak = jnp.maximum(old, jnp.max(score, axis=1, keepdims=True))
    weight = jnp.exp2(score - peak)
    decay = jnp.exp2(old - peak)
    whole = norm[:, :1] * decay + jnp.sum(weight, axis=1, keepdims=True)
    result = mix[...] * decay + jnp.dot(
        weight.astype(jnp.bfloat16), fresh_value.astype(jnp.bfloat16), preferred_element_type=jnp.float32
    )
    result = result / whole
    for r in range(rows):
        for h in range(heads):
            at = r * asks + h * steps
            attended_v[r, :, h * 128 : (h + 1) * 128] = result[at : at + steps].astype(jnp.bfloat16)
    store_attended = pltpu.make_async_copy(attended_v, attended.at[0], store_sem.at[1])
    store_attended.start()
    store_entries.wait()
    store_attended.wait()


def body(hidden, base_kv, delta_codes, delta_scales, queries, key_cache, value_cache, lengths):
    rows, steps, slab = hidden.shape[1:]
    owned, width = delta_codes.shape[1:]
    chunk = BLOCKS * owned
    context = key_cache.shape[3]
    query_width = queries.shape[3]
    tokens = rows * steps
    asks = rows * query_width // 128 * steps
    anywhere = pl.BlockSpec(memory_space=pl.ANY)
    scalars = pl.BlockSpec(memory_space=pltpu.SMEM)
    fast = pl.BlockSpec(memory_space=pltpu.VMEM)
    bf16, f32 = jnp.bfloat16, jnp.float32
    dma = pltpu.SemaphoreType.DMA
    middle = pl.pallas_call(
        exchange,
        out_shape=(
            pltpu.VMEM((tokens, width), f32),
            pltpu.VMEM((asks, 128), bf16),
            pltpu.VMEM((asks, 128), f32),
            pltpu.VMEM((asks, 128), f32),
            pltpu.VMEM((asks, 128), f32),
            pltpu.VMEM((tokens, 128), f32),
            pltpu.VMEM((tokens, 128), f32),
        ),
        in_specs=[anywhere] * 7 + [scalars],
        out_specs=[fast] * 7,
        scratch_shapes=[
            pltpu.VMEM((rows, steps, slab), bf16),
            pltpu.VMEM((rows, steps, query_width), bf16),
            pltpu.VMEM((BLOCKS, owned, width), bf16),
            pltpu.VMEM((BLOCKS, 2, owned), bf16),
            pltpu.VMEM((2, chunk, width), bf16),
            pltpu.VMEM((rows, context, 128), bf16),
            pltpu.VMEM((rows, context, 128), bf16),
            pltpu.VMEM((BLOCKS, owned, width), bf16),
            pltpu.VMEM((2, BLOCKS, owned, width), bf16),
            pltpu.VMEM((2, tokens, chunk), bf16),
            pltpu.VMEM((HALF, tokens, chunk), bf16),
            pltpu.VMEM((tokens, chunk), bf16),
            pltpu.VMEM((2, HALF, tokens, width), bf16),
            pltpu.VMEM((GROUPS, tokens, width), bf16),
            dma((5,)),
            dma((2, rows)),
            dma, dma, dma, dma, dma, dma, dma,
            dma((2,)), dma, dma, dma((6,)), dma, dma, pltpu.SemaphoreType.REGULAR,
        ],
        compiler_params=pltpu.CompilerParams(
            collective_id=0, has_side_effects=True, vmem_limit_bytes=60 * 1024 * 1024
        ),
    )(
        hidden, base_kv, delta_codes, jnp.transpose(delta_scales, (0, 2, 1)),
        queries, key_cache, value_cache, lengths,
    )
    return pl.pallas_call(
        finish,
        out_shape=(
            jax.ShapeDtypeStruct((1, rows, steps, width), bf16),
            jax.ShapeDtypeStruct((1, rows, steps, query_width), bf16),
        ),
        in_specs=[fast] * 7,
        out_specs=[anywhere, anywhere],
        scratch_shapes=[
            pltpu.VMEM((rows, steps, width), bf16),
            pltpu.VMEM((rows, steps, query_width), bf16),
            dma((2,)),
        ],
        compiler_params=pltpu.CompilerParams(vmem_limit_bytes=8 * 1024 * 1024),
    )(*middle)


def solution(mesh):
    placed = (
        P("section", "group", None, "tensor"),
        P(("section", "tensor"), None, None),
        P(None, ("group", "section", "tensor"), None),
        P(None, ("group", "section", "tensor"), None),
        P("section", "group", None, "tensor"),
        P("section", "group", "tensor", None, None),
        P("section", "group", "tensor", None, None),
        P("group"),
    )
    return jax.shard_map(
        body,
        mesh=mesh,
        in_specs=placed,
        out_specs=(P("section", "group", None, "tensor"), P("section", "group", None, "tensor")),
        check_vma=False,
    )
```

```python
import math

import jax
import jax.numpy as jnp
from jax import lax
from jax.experimental import pallas as pl
from jax.experimental.pallas import tpu as pltpu
from jax.sharding import PartitionSpec as P

MESH = pl.DeviceIdType.MESH
LOG2E = math.log2(math.e)
SCALE = 128 ** -0.5 * LOG2E
HIGH, WIDE, TENSORS, SECTIONS = 4, 4, 8, 2
GROUPS = HIGH * WIDE
BLOCKS = SECTIONS * TENSORS
HALF = GROUPS // 2


def exchange(
    hidden, base, codes, scales, queries, keys, values, lengths,
    projected, asked, best, norm, mix, cosine, sine,
    hidden_v, queries_v, codes_v, scales_v, base_v, keys_v, values_v,
    delta_out, delta_in, half_out, hidden_in, held, part_out, part_in,
    load_sem, cache_sem, delta_send, delta_recv, pass_send, pass_recv, base_send, base_recv,
    half_send, half_recv, held_recv, spread_send, spread_recv, part_send, part_recv, ready,
):
    g = lax.axis_index("group")
    s = lax.axis_index("section")
    t = lax.axis_index("tensor")
    me = s * TENSORS + t
    chip = lax.div(t, 2)
    core = lax.rem(t, 2)
    high = lax.div(g, WIDE)
    wide = lax.rem(g, WIDE)
    rows, steps = hidden_v.shape[0], hidden_v.shape[1]
    owned = codes_v.shape[1]
    chunk = BLOCKS * owned
    heads = queries_v.shape[2] // 128
    asks = heads * steps
    context = keys_v.shape[1]

    def at(og, os, ot):
        return {"group": og, "section": os, "tensor": ot}

    sibling = 2 * chip + 1 - core
    turns = (2, 1, 3, 0)
    inside = []
    for i in turns:
        for ds in (1, 0):
            for dc in (1, 0):
                if i or ds or dc:
                    os, ot = lax.rem(s + ds, 2), 2 * lax.rem(chip + i, 4) + lax.rem(core + dc, 2)
                    inside.append((os * TENSORS + ot, at(g, os, ot)))
    early = high < 2
    mirror = WIDE * (HIGH - 1 - high) + wide
    early_rows = 1 - core
    late_rows = 3 - core
    early_wide = lax.rem(chip + 2 * core, WIDE)
    late_wide = chip
    late_cores = [at(mirror, s, 2 * lax.rem(chip + i, 4) + core) for i in turns]
    barrier = pltpu.get_barrier_semaphore()

    @pl.when(early)
    def _():
        for og in (mirror, g):
            there = at(WIDE * early_rows + early_wide, s, lax.div(og, 2))
            pl.semaphore_signal(barrier, inc=1, device_id=there, device_id_type=MESH)
        for there in late_cores:
            pl.semaphore_signal(barrier, inc=1, device_id=there, device_id_type=MESH)

    there = at(WIDE * late_rows + late_wide, s, lax.div(g, 2))
    pl.semaphore_signal(barrier, inc=1, device_id=there, device_id_type=MESH)
    for _, there in inside:
        pl.semaphore_signal(barrier, inc=1, device_id=there, device_id_type=MESH)

    loads = [
        pltpu.make_async_copy(hidden.at[0], hidden_v, load_sem.at[0]),
        pltpu.make_async_copy(codes, codes_v, load_sem.at[1]),
        pltpu.make_async_copy(scales, scales_v, load_sem.at[2]),
        pltpu.make_async_copy(queries.at[0], queries_v, load_sem.at[3]),
        pltpu.make_async_copy(base.at[0, pl.ds(g * chunk, chunk), :], base_v.at[core], load_sem.at[4]),
    ]
    for load in loads:
        load.start()
    caches = []
    for r in range(rows):
        caches.append(
            (
                pltpu.make_async_copy(keys.at[0, r, 0], keys_v.at[r], cache_sem.at[0, r]),
                pltpu.make_async_copy(values.at[0, r, 0], values_v.at[r], cache_sem.at[1, r]),
            )
        )
        for load in caches[r]:
            load.start()

    loads[0].wait()
    slab = jnp.concatenate([hidden_v[r].astype(jnp.float32) for r in range(rows)], axis=0)
    for h in range(2):
        half_out[h] = slab[:, h * chunk : (h + 1) * chunk].astype(jnp.bfloat16)

    loads[1].wait()
    loads[2].wait()
    turned = scales_v[...].astype(jnp.float32).reshape(BLOCKS * 2, owned).T
    for b in range(BLOCKS):
        code = codes_v[b].astype(jnp.float32)
        left = code[:, :128] * turned[:, 2 * b : 2 * b + 1]
        right = code[:, 128:] * turned[:, 2 * b + 1 : 2 * b + 2]
        delta_out[b] = jnp.concatenate([left, right], axis=1).astype(jnp.bfloat16)

    pl.semaphore_wait(barrier, len(inside) + 2 + len(late_cores) * lax.div(high, 2))

    @pl.when(jnp.logical_not(early))
    def _():
        for i in range(4):
            pl.semaphore_signal(ready, inc=1, device_id=at(mirror, s, 2 * i + core), device_id_type=MESH)

    is_early = 1 - lax.div(high, 2)
    place_there = hidden_in.at[(1 - is_early) * WIDE + wide]
    relay_core = 1 - lax.rem(high, 2)
    relay_chip = lax.rem(wide + 2 * is_early * relay_core, WIDE)

    def half_copy(h, og, target, sem):
        return pltpu.make_async_remote_copy(
            src_ref=half_out.at[h],
            dst_ref=target,
            send_sem=half_send,
            recv_sem=sem,
            device_id=at(og, s, 2 * relay_chip + relay_core),
            device_id_type=MESH,
        )

    relayed = early & (chip >= 2)
    via = is_early * lax.div(chip, 2)
    half_to = [WIDE * ((1 - via) * chip + via * (HIGH - 1 - chip)) + 2 * core + h for h in range(2)]
    stays = [(og == g) & (2 * relay_chip + relay_core == t) for og in half_to]
    for h in range(2):
        for here_first, target, sem in (
            (jnp.logical_not(relayed), place_there, half_recv.at[1 - is_early]),
            (relayed, held, held_recv),
        ):

            @pl.when(here_first & stays[h])
            def _():
                pltpu.make_async_copy(half_out.at[h], target, sem).start()

            @pl.when(here_first & jnp.logical_not(stays[h]))
            def _():
                half_copy(h, half_to[h], target, sem).start()

    for other, there in inside:
        pltpu.make_async_remote_copy(
            src_ref=delta_out.at[other],
            dst_ref=delta_in.at[lax.rem(other, 2), me],
            send_sem=delta_send,
            recv_sem=delta_recv,
            device_id=there,
            device_id_type=MESH,
        ).start()
    pltpu.make_async_copy(delta_out.at[me], delta_in.at[core, me], delta_recv).start()

    loads[4].wait()
    base_copy = pltpu.make_async_remote_copy(
        src_ref=base_v.at[core],
        dst_ref=base_v.at[core],
        send_sem=base_send,
        recv_sem=base_recv,
        device_id=at(g, s, sibling),
        device_id_type=MESH,
    )
    base_copy.start()

    loads[3].wait()
    for r in range(rows):
        block = queries_v[r].astype(jnp.float32)
        asked[pl.ds(r * asks, asks), :] = jnp.concatenate(
            [block[:, h * 128 : (h + 1) * 128] for h in range(heads)], axis=0
        ).astype(jnp.bfloat16)

    def attend(r):
        lines = pl.ds(r * asks, asks)
        caches[r][0].wait()
        score = lax.dot_general(
            asked[lines, :], keys_v[r], (((1,), (1,)), ((), ())), preferred_element_type=jnp.float32
        ) * SCALE
        place = lax.broadcasted_iota(jnp.int32, (asks, context), 1)
        score = jnp.where(place < lengths[r], score, -jnp.inf)
        peak = jnp.max(score, axis=1, keepdims=True)
        weight = jnp.exp2(score - peak)
        total = jnp.sum(weight, axis=1, keepdims=True)
        caches[r][1].wait()
        best[lines, :] = jnp.broadcast_to(peak, (asks, 128))
        norm[lines, :] = jnp.broadcast_to(total, (asks, 128))
        mix[lines, :] = jnp.dot(weight.astype(jnp.bfloat16), values_v[r], preferred_element_type=jnp.float32)

    attend(0)
    attend(1)

    early_piece = hidden_in.at[early_wide]
    late_piece = hidden_in.at[WIDE + late_wide]

    def spread_copy(piece, sem, i):
        return pltpu.make_async_remote_copy(
            src_ref=piece,
            dst_ref=piece,
            send_sem=spread_send,
            recv_sem=spread_recv.at[sem],
            device_id=at(g, s, 2 * lax.rem(chip + i, 4) + core),
            device_id_type=MESH,
        )

    def relay_copy(there):
        return pltpu.make_async_remote_copy(
            src_ref=held,
            dst_ref=early_piece,
            send_sem=spread_send,
            recv_sem=spread_recv.at[early_wide],
            device_id=there,
            device_id_type=MESH,
        )

    @pl.when(early)
    def _():
        pltpu.make_async_copy(early_piece, early_piece, half_recv.at[0]).wait()
        for i in turns[:3]:
            spread_copy(early_piece, early_wide, i).start()
        pl.semaphore_wait(ready, len(late_cores))
        pltpu.make_async_copy(held, held, held_recv).wait()
        for there in late_cores:
            relay_copy(there).start()

    attend(2)

    mine = delta_in.at[core]
    pltpu.make_async_copy(mine, mine, delta_recv).wait()
    pass_copy = pltpu.make_async_remote_copy(
        src_ref=mine,
        dst_ref=mine,
        send_sem=pass_send,
        recv_sem=pass_recv,
        device_id=at(g, s, sibling),
        device_id_type=MESH,
    )
    pass_copy.start()

    pltpu.make_async_copy(late_piece, late_piece, half_recv.at[1]).wait()
    for i in turns[:3]:
        spread_copy(late_piece, WIDE + late_wide, i).start()

    base_copy.wait_recv()
    pass_copy.wait_recv()
    tokens = rows * steps

    def send_part(c, slot, og):
        return pltpu.make_async_remote_copy(
            src_ref=part_out.at[c, slot],
            dst_ref=part_in.at[g],
            send_sem=part_send,
            recv_sem=part_recv,
            device_id=at(og, s, 2 * chip + c),
            device_id_type=MESH,
        )

    sends = []
    for phase, oh in enumerate((early_rows, late_rows)):
        for j in range(WIDE):
            taken_here = (early & (early_wide == j)) if phase == 0 else (late_wide == j)

            @pl.when(jnp.logical_not(taken_here))
            def _():
                piece = hidden_in.at[phase * WIDE + j]
                pltpu.make_async_copy(piece, piece, spread_recv.at[phase * WIDE + j]).wait()

        slots = pl.ds(phase * WIDE, WIDE)
        features = hidden_in[slots].reshape(WIDE * tokens, chunk)
        for c in (1, 0):
            part = jnp.dot(features, base_v[c], preferred_element_type=jnp.float32)
            part = part + jnp.dot(
                features, delta_in[c].reshape(chunk, part.shape[1]), preferred_element_type=jnp.float32
            )
            part_out[c, slots] = part.reshape(WIDE, tokens, part.shape[1]).astype(jnp.bfloat16)
            for j in range(WIDE):
                slot = phase * WIDE + j
                og = WIDE * oh + j
                sends.append((c, slot, og))
                local = (og == g) & (core == c)

                @pl.when(local)
                def _():
                    pltpu.make_async_copy(part_out.at[c, slot], part_in.at[g], part_recv).start()

                @pl.when(jnp.logical_not(local))
                def _():
                    send_part(c, slot, og).start()

    attend(3)

    line = lax.broadcasted_iota(jnp.int32, (tokens, 128), 0)
    lane = lax.broadcasted_iota(jnp.int32, (tokens, 128), 1)
    start = jnp.zeros((tokens, 128), jnp.int32)
    for r in range(rows):
        start = jnp.where(line // steps == r, lengths[r], start)
    position = (start + line % steps).astype(jnp.float32)
    frequency = jnp.exp((lane % 64).astype(jnp.float32) * (-2.0 * math.log(1000000.0) / 128))
    phase = position * frequency
    cosine[...] = jnp.cos(phase)
    turned_sine = jnp.sin(phase)
    sine[...] = jnp.where(lane < 64, -turned_sine, turned_sine)

    for h in range(2):

        @pl.when(jnp.logical_not(stays[h]))
        def _():
            half_copy(h, g, place_there, half_recv.at[0]).wait_send()

    for i in turns[:3]:
        spread_copy(late_piece, WIDE + late_wide, i).wait_send()

    @pl.when(early)
    def _():
        for i in turns[:3]:
            spread_copy(early_piece, early_wide, i).wait_send()
        for there in late_cores:
            relay_copy(there).wait_send()

    sent = delta_out.at[pl.ds(0, BLOCKS - 1)]
    pltpu.make_async_copy(sent, sent, delta_send).wait()
    base_copy.wait_send()
    pass_copy.wait_send()
    for c, slot, og in sends:

        @pl.when(jnp.logical_not((og == g) & (core == c)))
        def _():
            send_part(c, slot, og).wait_send()

    pltpu.make_async_copy(part_in, part_in, part_recv).wait()
    projected[...] = jnp.sum(part_in[...].astype(jnp.float32), axis=0)


def finish(projected, asked, best, norm, mix, cosine, sine, entries, attended, entries_v, attended_v, store_sem):
    rows, steps = entries_v.shape[0], entries_v.shape[1]
    tokens = rows * steps
    total = asked.shape[0]
    asks = total // rows
    heads = asks // steps

    key = projected[:, :128]
    swapped = jnp.concatenate([key[:, 64:], key[:, :64]], axis=1)
    fresh_key = key * cosine[...] + swapped * sine[...]
    fresh_value = projected[:, 128:]
    for r in range(rows):
        lines = slice(r * steps, (r + 1) * steps)
        entries_v[r] = jnp.concatenate([fresh_key[lines], fresh_value[lines]], axis=1).astype(jnp.bfloat16)
    store_entries = pltpu.make_async_copy(entries_v, entries.at[0], store_sem.at[0])
    store_entries.start()

    score = lax.dot_general(
        asked[...], fresh_key.astype(jnp.bfloat16), (((1,), (1,)), ((), ())), preferred_element_type=jnp.float32
    ) * SCALE
    line = lax.broadcasted_iota(jnp.int32, (total, tokens), 0)
    col = lax.broadcasted_iota(jnp.int32, (total, tokens), 1)
    seen = (line // asks == col // steps) & (col % steps <= line % steps)
    score = jnp.where(seen, score, -jnp.inf)
    old = best[:, :1]
    peak = jnp.maximum(old, jnp.max(score, axis=1, keepdims=True))
    weight = jnp.exp2(score - peak)
    decay = jnp.exp2(old - peak)
    whole = norm[:, :1] * decay + jnp.sum(weight, axis=1, keepdims=True)
    result = mix[...] * decay + jnp.dot(
        weight.astype(jnp.bfloat16), fresh_value.astype(jnp.bfloat16), preferred_element_type=jnp.float32
    )
    result = result / whole
    for r in range(rows):
        for h in range(heads):
            at = r * asks + h * steps
            attended_v[r, :, h * 128 : (h + 1) * 128] = result[at : at + steps].astype(jnp.bfloat16)
    store_attended = pltpu.make_async_copy(attended_v, attended.at[0], store_sem.at[1])
    store_attended.start()
    store_entries.wait()
    store_attended.wait()


def body(hidden, base_kv, delta_codes, delta_scales, queries, key_cache, value_cache, lengths):
    rows, steps, slab = hidden.shape[1:]
    owned, width = delta_codes.shape[1:]
    chunk = BLOCKS * owned
    context = key_cache.shape[3]
    query_width = queries.shape[3]
    tokens = rows * steps
    asks = rows * query_width // 128 * steps
    anywhere = pl.BlockSpec(memory_space=pl.ANY)
    scalars = pl.BlockSpec(memory_space=pltpu.SMEM)
    fast = pl.BlockSpec(memory_space=pltpu.VMEM)
    bf16, f32 = jnp.bfloat16, jnp.float32
    dma = pltpu.SemaphoreType.DMA
    middle = pl.pallas_call(
        exchange,
        out_shape=(
            pltpu.VMEM((tokens, width), f32),
            pltpu.VMEM((asks, 128), bf16),
            pltpu.VMEM((asks, 128), f32),
            pltpu.VMEM((asks, 128), f32),
            pltpu.VMEM((asks, 128), f32),
            pltpu.VMEM((tokens, 128), f32),
            pltpu.VMEM((tokens, 128), f32),
        ),
        in_specs=[anywhere] * 7 + [scalars],
        out_specs=[fast] * 7,
        scratch_shapes=[
            pltpu.VMEM((rows, steps, slab), bf16),
            pltpu.VMEM((rows, steps, query_width), bf16),
            pltpu.VMEM((BLOCKS, owned, width), bf16),
            pltpu.VMEM((BLOCKS, 2, owned), bf16),
            pltpu.VMEM((2, chunk, width), bf16),
            pltpu.VMEM((rows, context, 128), bf16),
            pltpu.VMEM((rows, context, 128), bf16),
            pltpu.VMEM((BLOCKS, owned, width), bf16),
            pltpu.VMEM((2, BLOCKS, owned, width), bf16),
            pltpu.VMEM((2, tokens, chunk), bf16),
            pltpu.VMEM((HALF, tokens, chunk), bf16),
            pltpu.VMEM((tokens, chunk), bf16),
            pltpu.VMEM((2, HALF, tokens, width), bf16),
            pltpu.VMEM((GROUPS, tokens, width), bf16),
            dma((5,)),
            dma((2, rows)),
            dma, dma, dma, dma, dma, dma, dma,
            dma((2,)), dma, dma, dma((2 * WIDE,)), dma, dma, pltpu.SemaphoreType.REGULAR,
        ],
        compiler_params=pltpu.CompilerParams(
            collective_id=0, has_side_effects=True, vmem_limit_bytes=60 * 1024 * 1024
        ),
    )(
        hidden, base_kv, delta_codes, jnp.transpose(delta_scales, (0, 2, 1)),
        queries, key_cache, value_cache, lengths,
    )
    return pl.pallas_call(
        finish,
        out_shape=(
            jax.ShapeDtypeStruct((1, rows, steps, width), bf16),
            jax.ShapeDtypeStruct((1, rows, steps, query_width), bf16),
        ),
        in_specs=[fast] * 7,
        out_specs=[anywhere, anywhere],
        scratch_shapes=[
            pltpu.VMEM((rows, steps, width), bf16),
            pltpu.VMEM((rows, steps, query_width), bf16),
            dma((2,)),
        ],
        compiler_params=pltpu.CompilerParams(vmem_limit_bytes=8 * 1024 * 1024),
    )(*middle)


def solution(mesh):
    placed = (
        P("section", "group", None, "tensor"),
        P(("section", "tensor"), None, None),
        P(None, ("group", "section", "tensor"), None),
        P(None, ("group", "section", "tensor"), None),
        P("section", "group", None, "tensor"),
        P("section", "group", "tensor", None, None),
        P("section", "group", "tensor", None, None),
        P("group"),
    )
    return jax.shard_map(
        body,
        mesh=mesh,
        in_specs=placed,
        out_specs=(P("section", "group", None, "tensor"), P("section", "group", None, "tensor")),
        check_vma=False,
    )
```

```python
import math

import jax
import jax.numpy as jnp
from jax import lax
from jax.experimental import pallas as pl
from jax.experimental.pallas import tpu as pltpu
from jax.sharding import PartitionSpec as P

MESH = pl.DeviceIdType.MESH
LOG2E = math.log2(math.e)
SCALE = 128 ** -0.5 * LOG2E
HIGH, WIDE, TENSORS, SECTIONS = 4, 4, 8, 2
GROUPS = HIGH * WIDE
BLOCKS = SECTIONS * TENSORS
HALF = GROUPS // 2


def exchange(
    hidden, base, codes, scales, queries, keys, values, lengths,
    projected, asked, best, norm, mix, cosine, sine,
    hidden_v, queries_v, codes_v, scales_v, base_v, keys_v, values_v,
    delta_out, delta_in, half_out, hidden_in, held, part_out, part_in,
    load_sem, cache_sem, delta_send, delta_recv, pass_send, pass_recv, base_send, base_recv,
    half_send, half_recv, held_recv, spread_send, spread_recv, part_send, part_recv, ready,
):
    g = lax.axis_index("group")
    s = lax.axis_index("section")
    t = lax.axis_index("tensor")
    me = s * TENSORS + t
    chip = lax.div(t, 2)
    core = lax.rem(t, 2)
    high = lax.div(g, WIDE)
    wide = lax.rem(g, WIDE)
    rows, steps = hidden_v.shape[0], hidden_v.shape[1]
    owned = codes_v.shape[1]
    chunk = BLOCKS * owned
    heads = queries_v.shape[2] // 128
    asks = heads * steps
    context = keys_v.shape[1]

    def at(og, os, ot):
        return {"group": og, "section": os, "tensor": ot}

    sibling = 2 * chip + 1 - core
    turns = (2, 1, 3, 0)
    inside = []
    for i in turns:
        for ds in (1, 0):
            for dc in (1, 0):
                if i or ds or dc:
                    os, ot = lax.rem(s + ds, 2), 2 * lax.rem(chip + i, 4) + lax.rem(core + dc, 2)
                    inside.append((os * TENSORS + ot, at(g, os, ot)))
    early = high < 2
    mirror = WIDE * (HIGH - 1 - high) + wide
    early_rows = 1 - core
    late_rows = 3 - core
    early_wide = lax.rem(chip + 2 * core, WIDE)
    late_wide = chip
    relays = ((early & (s * core * high == 0), mirror), ((high == 0) & (s * core == 1), 2 * WIDE + wide))

    def late_cores(og):
        return [at(og, s, 2 * lax.rem(chip + i, 4) + core) for i in turns]

    barrier = pltpu.get_barrier_semaphore()

    def early_source(og):
        return at(WIDE * early_rows + early_wide, s, lax.div(og, 2))

    for does, og in relays:

        @pl.when(does)
        def _():
            pl.semaphore_signal(barrier, inc=1, device_id=early_source(og), device_id_type=MESH)
            for there in late_cores(og):
                pl.semaphore_signal(barrier, inc=1, device_id=there, device_id_type=MESH)

    @pl.when(early)
    def _():
        pl.semaphore_signal(barrier, inc=1, device_id=early_source(g), device_id_type=MESH)

    there = at(WIDE * late_rows + late_wide, s, lax.div(g, 2))
    pl.semaphore_signal(barrier, inc=1, device_id=there, device_id_type=MESH)
    for _, there in inside:
        pl.semaphore_signal(barrier, inc=1, device_id=there, device_id_type=MESH)

    loads = [
        pltpu.make_async_copy(hidden.at[0], hidden_v, load_sem.at[0]),
        pltpu.make_async_copy(codes, codes_v, load_sem.at[1]),
        pltpu.make_async_copy(scales, scales_v, load_sem.at[2]),
        pltpu.make_async_copy(queries.at[0], queries_v, load_sem.at[3]),
        pltpu.make_async_copy(base.at[0, pl.ds(g * chunk, chunk), :], base_v.at[core], load_sem.at[4]),
    ]
    for load in loads:
        load.start()
    caches = []
    for r in range(rows):
        caches.append(
            (
                pltpu.make_async_copy(keys.at[0, r, 0], keys_v.at[r], cache_sem.at[0, r]),
                pltpu.make_async_copy(values.at[0, r, 0], values_v.at[r], cache_sem.at[1, r]),
            )
        )
        for load in caches[r]:
            load.start()

    loads[0].wait()
    slab = jnp.concatenate([hidden_v[r].astype(jnp.float32) for r in range(rows)], axis=0)
    for h in range(2):
        half_out[h] = slab[:, h * chunk : (h + 1) * chunk].astype(jnp.bfloat16)

    loads[1].wait()
    loads[2].wait()
    turned = scales_v[...].astype(jnp.float32).reshape(BLOCKS * 2, owned).T
    for b in range(BLOCKS):
        code = codes_v[b].astype(jnp.float32)
        left = code[:, :128] * turned[:, 2 * b : 2 * b + 1]
        right = code[:, 128:] * turned[:, 2 * b + 1 : 2 * b + 2]
        delta_out[b] = jnp.concatenate([left, right], axis=1).astype(jnp.bfloat16)

    pl.semaphore_wait(barrier, len(inside) + 2 + 4 * lax.div(high, 2))

    @pl.when(jnp.logical_not(early))
    def _():
        which = s * core * (HIGH - 1 - high)
        og = WIDE * (HIGH - 1 - high) * (1 - s * core) + wide
        for i in range(4):
            there = at(og, s, 2 * i + core)
            pl.semaphore_signal(ready.at[which], inc=1, device_id=there, device_id_type=MESH)

    is_early = 1 - lax.div(high, 2)
    place_there = hidden_in.at[(1 - is_early) * WIDE + wide]
    relay_core = 1 - lax.rem(high, 2)
    relay_chip = lax.rem(wide + 2 * is_early * relay_core, WIDE)

    def half_copy(h, og, target, sem):
        return pltpu.make_async_remote_copy(
            src_ref=half_out.at[h],
            dst_ref=target,
            send_sem=half_send,
            recv_sem=sem,
            device_id=at(og, s, 2 * relay_chip + relay_core),
            device_id_type=MESH,
        )

    relayed = early & (chip >= 2)
    via = is_early * lax.div(chip, 2)
    which_held = via * s * (1 - high) * (HIGH - 1 - chip)
    half_to = [WIDE * ((1 - via) * chip + via * (1 - s * (1 - high)) * (HIGH - 1 - chip)) + 2 * core + h for h in range(2)]
    stays = [(og == g) & (2 * relay_chip + relay_core == t) for og in half_to]
    for h in range(2):
        for here_first, target, sem in (
            (jnp.logical_not(relayed), place_there, half_recv.at[1 - is_early]),
            (relayed, held.at[which_held], held_recv.at[which_held]),
        ):

            @pl.when(here_first & stays[h])
            def _():
                pltpu.make_async_copy(half_out.at[h], target, sem).start()

            @pl.when(here_first & jnp.logical_not(stays[h]))
            def _():
                half_copy(h, half_to[h], target, sem).start()

    for other, there in inside:
        pltpu.make_async_remote_copy(
            src_ref=delta_out.at[other],
            dst_ref=delta_in.at[lax.rem(other, 2), me],
            send_sem=delta_send,
            recv_sem=delta_recv,
            device_id=there,
            device_id_type=MESH,
        ).start()
    pltpu.make_async_copy(delta_out.at[me], delta_in.at[core, me], delta_recv).start()

    loads[4].wait()
    base_copy = pltpu.make_async_remote_copy(
        src_ref=base_v.at[core],
        dst_ref=base_v.at[core],
        send_sem=base_send,
        recv_sem=base_recv,
        device_id=at(g, s, sibling),
        device_id_type=MESH,
    )
    base_copy.start()

    loads[3].wait()
    for r in range(rows):
        block = queries_v[r].astype(jnp.float32)
        asked[pl.ds(r * asks, asks), :] = jnp.concatenate(
            [block[:, h * 128 : (h + 1) * 128] for h in range(heads)], axis=0
        ).astype(jnp.bfloat16)

    def attend(r):
        lines = pl.ds(r * asks, asks)
        caches[r][0].wait()
        score = lax.dot_general(
            asked[lines, :], keys_v[r], (((1,), (1,)), ((), ())), preferred_element_type=jnp.float32
        ) * SCALE
        place = lax.broadcasted_iota(jnp.int32, (asks, context), 1)
        score = jnp.where(place < lengths[r], score, -jnp.inf)
        peak = jnp.max(score, axis=1, keepdims=True)
        weight = jnp.exp2(score - peak)
        total = jnp.sum(weight, axis=1, keepdims=True)
        caches[r][1].wait()
        best[lines, :] = jnp.broadcast_to(peak, (asks, 128))
        norm[lines, :] = jnp.broadcast_to(total, (asks, 128))
        mix[lines, :] = jnp.dot(weight.astype(jnp.bfloat16), values_v[r], preferred_element_type=jnp.float32)

    attend(0)
    attend(1)

    early_piece = hidden_in.at[early_wide]
    late_piece = hidden_in.at[WIDE + late_wide]

    def spread_copy(piece, sem, i):
        return pltpu.make_async_remote_copy(
            src_ref=piece,
            dst_ref=piece,
            send_sem=spread_send,
            recv_sem=spread_recv.at[sem],
            device_id=at(g, s, 2 * lax.rem(chip + i, 4) + core),
            device_id_type=MESH,
        )

    def relay_copy(k, there):
        return pltpu.make_async_remote_copy(
            src_ref=held.at[k],
            dst_ref=early_piece,
            send_sem=spread_send,
            recv_sem=spread_recv.at[early_wide],
            device_id=there,
            device_id_type=MESH,
        )

    @pl.when(early)
    def _():
        pltpu.make_async_copy(early_piece, early_piece, half_recv.at[0]).wait()
        for i in turns[:3]:
            spread_copy(early_piece, early_wide, i).start()

    for k in (1, 0):
        does, og = relays[k]

        @pl.when(does)
        def _():
            pl.semaphore_wait(ready.at[k], 4)
            pltpu.make_async_copy(held.at[k], held.at[k], held_recv.at[k]).wait()
            for there in late_cores(og):
                relay_copy(k, there).start()

    attend(2)

    mine = delta_in.at[core]
    pltpu.make_async_copy(mine, mine, delta_recv).wait()
    pass_copy = pltpu.make_async_remote_copy(
        src_ref=mine,
        dst_ref=mine,
        send_sem=pass_send,
        recv_sem=pass_recv,
        device_id=at(g, s, sibling),
        device_id_type=MESH,
    )
    pass_copy.start()

    pltpu.make_async_copy(late_piece, late_piece, half_recv.at[1]).wait()
    for i in turns[:3]:
        spread_copy(late_piece, WIDE + late_wide, i).start()

    base_copy.wait_recv()
    pass_copy.wait_recv()
    tokens = rows * steps

    def send_part(c, slot, og):
        return pltpu.make_async_remote_copy(
            src_ref=part_out.at[c, slot],
            dst_ref=part_in.at[g],
            send_sem=part_send,
            recv_sem=part_recv,
            device_id=at(og, s, 2 * chip + c),
            device_id_type=MESH,
        )

    sends = []
    for phase, taken in ((0, (0, 1)), (0, (2, 3)), (1, (0, 1, 2, 3))):
        oh = (early_rows, late_rows)[phase]
        for j in taken:
            taken_here = (early & (early_wide == j)) if phase == 0 else (late_wide == j)

            @pl.when(jnp.logical_not(taken_here))
            def _():
                piece = hidden_in.at[phase * WIDE + j]
                pltpu.make_async_copy(piece, piece, spread_recv.at[phase * WIDE + j]).wait()

        slots = pl.ds(phase * WIDE + taken[0], len(taken))
        features = hidden_in[slots].reshape(len(taken) * tokens, chunk)
        for c in (1, 0):
            part = jnp.dot(features, base_v[c], preferred_element_type=jnp.float32)
            part = part + jnp.dot(
                features, delta_in[c].reshape(chunk, part.shape[1]), preferred_element_type=jnp.float32
            )
            part_out[c, slots] = part.reshape(len(taken), tokens, part.shape[1]).astype(jnp.bfloat16)
            for j in taken:
                slot = phase * WIDE + j
                og = WIDE * oh + j
                sends.append((c, slot, og))
                local = (og == g) & (core == c)

                @pl.when(local)
                def _():
                    pltpu.make_async_copy(part_out.at[c, slot], part_in.at[g], part_recv).start()

                @pl.when(jnp.logical_not(local))
                def _():
                    send_part(c, slot, og).start()

    attend(3)

    line = lax.broadcasted_iota(jnp.int32, (tokens, 128), 0)
    lane = lax.broadcasted_iota(jnp.int32, (tokens, 128), 1)
    start = jnp.zeros((tokens, 128), jnp.int32)
    for r in range(rows):
        start = jnp.where(line // steps == r, lengths[r], start)
    position = (start + line % steps).astype(jnp.float32)
    frequency = jnp.exp((lane % 64).astype(jnp.float32) * (-2.0 * math.log(1000000.0) / 128))
    phase = position * frequency
    cosine[...] = jnp.cos(phase)
    turned_sine = jnp.sin(phase)
    sine[...] = jnp.where(lane < 64, -turned_sine, turned_sine)

    for h in range(2):

        @pl.when(jnp.logical_not(stays[h]))
        def _():
            half_copy(h, g, place_there, half_recv.at[0]).wait_send()

    for i in turns[:3]:
        spread_copy(late_piece, WIDE + late_wide, i).wait_send()

    @pl.when(early)
    def _():
        for i in turns[:3]:
            spread_copy(early_piece, early_wide, i).wait_send()

    for k, (does, og) in enumerate(relays):

        @pl.when(does)
        def _():
            for there in late_cores(og):
                relay_copy(k, there).wait_send()

    sent = delta_out.at[pl.ds(0, BLOCKS - 1)]
    pltpu.make_async_copy(sent, sent, delta_send).wait()
    base_copy.wait_send()
    pass_copy.wait_send()
    for c, slot, og in sends:

        @pl.when(jnp.logical_not((og == g) & (core == c)))
        def _():
            send_part(c, slot, og).wait_send()

    pltpu.make_async_copy(part_in, part_in, part_recv).wait()
    projected[...] = jnp.sum(part_in[...].astype(jnp.float32), axis=0)


def finish(projected, asked, best, norm, mix, cosine, sine, entries, attended, entries_v, attended_v, store_sem):
    rows, steps = entries_v.shape[0], entries_v.shape[1]
    tokens = rows * steps
    total = asked.shape[0]
    asks = total // rows
    heads = asks // steps

    key = projected[:, :128]
    swapped = jnp.concatenate([key[:, 64:], key[:, :64]], axis=1)
    fresh_key = key * cosine[...] + swapped * sine[...]
    fresh_value = projected[:, 128:]
    for r in range(rows):
        lines = slice(r * steps, (r + 1) * steps)
        entries_v[r] = jnp.concatenate([fresh_key[lines], fresh_value[lines]], axis=1).astype(jnp.bfloat16)
    store_entries = pltpu.make_async_copy(entries_v, entries.at[0], store_sem.at[0])
    store_entries.start()

    score = lax.dot_general(
        asked[...], fresh_key.astype(jnp.bfloat16), (((1,), (1,)), ((), ())), preferred_element_type=jnp.float32
    ) * SCALE
    line = lax.broadcasted_iota(jnp.int32, (total, tokens), 0)
    col = lax.broadcasted_iota(jnp.int32, (total, tokens), 1)
    seen = (line // asks == col // steps) & (col % steps <= line % steps)
    score = jnp.where(seen, score, -jnp.inf)
    old = best[:, :1]
    peak = jnp.maximum(old, jnp.max(score, axis=1, keepdims=True))
    weight = jnp.exp2(score - peak)
    decay = jnp.exp2(old - peak)
    whole = norm[:, :1] * decay + jnp.sum(weight, axis=1, keepdims=True)
    result = mix[...] * decay + jnp.dot(
        weight.astype(jnp.bfloat16), fresh_value.astype(jnp.bfloat16), preferred_element_type=jnp.float32
    )
    result = result / whole
    for r in range(rows):
        for h in range(heads):
            at = r * asks + h * steps
            attended_v[r, :, h * 128 : (h + 1) * 128] = result[at : at + steps].astype(jnp.bfloat16)
    store_attended = pltpu.make_async_copy(attended_v, attended.at[0], store_sem.at[1])
    store_attended.start()
    store_entries.wait()
    store_attended.wait()


def body(hidden, base_kv, delta_codes, delta_scales, queries, key_cache, value_cache, lengths):
    rows, steps, slab = hidden.shape[1:]
    owned, width = delta_codes.shape[1:]
    chunk = BLOCKS * owned
    context = key_cache.shape[3]
    query_width = queries.shape[3]
    tokens = rows * steps
    asks = rows * query_width // 128 * steps
    anywhere = pl.BlockSpec(memory_space=pl.ANY)
    scalars = pl.BlockSpec(memory_space=pltpu.SMEM)
    fast = pl.BlockSpec(memory_space=pltpu.VMEM)
    bf16, f32 = jnp.bfloat16, jnp.float32
    dma = pltpu.SemaphoreType.DMA
    middle = pl.pallas_call(
        exchange,
        out_shape=(
            pltpu.VMEM((tokens, width), f32),
            pltpu.VMEM((asks, 128), bf16),
            pltpu.VMEM((asks, 128), f32),
            pltpu.VMEM((asks, 128), f32),
            pltpu.VMEM((asks, 128), f32),
            pltpu.VMEM((tokens, 128), f32),
            pltpu.VMEM((tokens, 128), f32),
        ),
        in_specs=[anywhere] * 7 + [scalars],
        out_specs=[fast] * 7,
        scratch_shapes=[
            pltpu.VMEM((rows, steps, slab), bf16),
            pltpu.VMEM((rows, steps, query_width), bf16),
            pltpu.VMEM((BLOCKS, owned, width), bf16),
            pltpu.VMEM((BLOCKS, 2, owned), bf16),
            pltpu.VMEM((2, chunk, width), bf16),
            pltpu.VMEM((rows, context, 128), bf16),
            pltpu.VMEM((rows, context, 128), bf16),
            pltpu.VMEM((BLOCKS, owned, width), bf16),
            pltpu.VMEM((2, BLOCKS, owned, width), bf16),
            pltpu.VMEM((2, tokens, chunk), bf16),
            pltpu.VMEM((HALF, tokens, chunk), bf16),
            pltpu.VMEM((2, tokens, chunk), bf16),
            pltpu.VMEM((2, HALF, tokens, width), bf16),
            pltpu.VMEM((GROUPS, tokens, width), bf16),
            dma((5,)),
            dma((2, rows)),
            dma, dma, dma, dma, dma, dma, dma,
            dma((2,)), dma((2,)), dma, dma((2 * WIDE,)), dma, dma, pltpu.SemaphoreType.REGULAR((2,)),
        ],
        compiler_params=pltpu.CompilerParams(
            collective_id=0, has_side_effects=True, vmem_limit_bytes=60 * 1024 * 1024
        ),
    )(
        hidden, base_kv, delta_codes, jnp.transpose(delta_scales, (0, 2, 1)),
        queries, key_cache, value_cache, lengths,
    )
    return pl.pallas_call(
        finish,
        out_shape=(
            jax.ShapeDtypeStruct((1, rows, steps, width), bf16),
            jax.ShapeDtypeStruct((1, rows, steps, query_width), bf16),
        ),
        in_specs=[fast] * 7,
        out_specs=[anywhere, anywhere],
        scratch_shapes=[
            pltpu.VMEM((rows, steps, width), bf16),
            pltpu.VMEM((rows, steps, query_width), bf16),
            dma((2,)),
        ],
        compiler_params=pltpu.CompilerParams(vmem_limit_bytes=8 * 1024 * 1024),
    )(*middle)


def solution(mesh):
    placed = (
        P("section", "group", None, "tensor"),
        P(("section", "tensor"), None, None),
        P(None, ("group", "section", "tensor"), None),
        P(None, ("group", "section", "tensor"), None),
        P("section", "group", None, "tensor"),
        P("section", "group", "tensor", None, None),
        P("section", "group", "tensor", None, None),
        P("group"),
    )
    return jax.shard_map(
        body,
        mesh=mesh,
        in_specs=placed,
        out_specs=(P("section", "group", None, "tensor"), P("section", "group", None, "tensor")),
        check_vma=False,
    )
```

```python
import math

import jax
import jax.numpy as jnp
from jax import lax
from jax.experimental import pallas as pl
from jax.experimental.pallas import tpu as pltpu
from jax.sharding import PartitionSpec as P

MESH = pl.DeviceIdType.MESH
LOG2E = math.log2(math.e)
SCALE = 128 ** -0.5 * LOG2E
HIGH, WIDE, TENSORS, SECTIONS = 4, 4, 8, 2
GROUPS = HIGH * WIDE
BLOCKS = SECTIONS * TENSORS
HALF = GROUPS // 2


def exchange(
    hidden, base, codes, scales, queries, keys, values, lengths,
    projected, asked, best, norm, mix, cosine, sine,
    hidden_v, queries_v, codes_v, scales_v, base_v, keys_v, values_v,
    delta_out, delta_in, half_out, hidden_in, held, part_out, part_in,
    load_sem, cache_sem, delta_send, delta_recv, pass_send, pass_recv, base_send, base_recv,
    half_send, half_recv, held_recv, spread_send, spread_recv, part_send, part_recv, ready,
):
    g = lax.axis_index("group")
    s = lax.axis_index("section")
    t = lax.axis_index("tensor")
    me = s * TENSORS + t
    chip = lax.div(t, 2)
    core = lax.rem(t, 2)
    high = lax.div(g, WIDE)
    wide = lax.rem(g, WIDE)
    rows, steps = hidden_v.shape[0], hidden_v.shape[1]
    owned = codes_v.shape[1]
    chunk = BLOCKS * owned
    heads = queries_v.shape[2] // 128
    asks = heads * steps
    context = keys_v.shape[1]

    def at(og, os, ot):
        return {"group": og, "section": os, "tensor": ot}

    sibling = 2 * chip + 1 - core
    turns = (2, 1, 3, 0)
    inside = []
    for i in turns:
        for ds in (1, 0):
            for dc in (1, 0):
                if i or ds or dc:
                    os, ot = lax.rem(s + ds, 2), 2 * lax.rem(chip + i, 4) + lax.rem(core + dc, 2)
                    inside.append((os * TENSORS + ot, at(g, os, ot)))
    early = high < 2
    mirror = WIDE * (HIGH - 1 - high) + wide
    early_rows = 1 - core
    late_rows = 3 - core
    early_wide = lax.rem(chip + 2 * core, WIDE)
    late_wide = chip
    relays = ((early & (s * core * high == 0), mirror), ((high == 0) & (s * core == 1), 2 * WIDE + wide))

    def late_cores(og):
        return [at(og, s, 2 * lax.rem(chip + i, 4) + core) for i in turns]

    barrier = pltpu.get_barrier_semaphore()

    def early_source(og):
        return at(WIDE * early_rows + early_wide, s, lax.div(og, 2))

    for does, og in relays:

        @pl.when(does)
        def _():
            pl.semaphore_signal(barrier, inc=1, device_id=early_source(og), device_id_type=MESH)
            for there in late_cores(og):
                pl.semaphore_signal(barrier, inc=1, device_id=there, device_id_type=MESH)

    @pl.when(early)
    def _():
        pl.semaphore_signal(barrier, inc=1, device_id=early_source(g), device_id_type=MESH)

    there = at(WIDE * late_rows + late_wide, s, lax.div(g, 2))
    pl.semaphore_signal(barrier, inc=1, device_id=there, device_id_type=MESH)
    for _, there in inside:
        pl.semaphore_signal(barrier, inc=1, device_id=there, device_id_type=MESH)

    loads = [
        pltpu.make_async_copy(hidden.at[0], hidden_v, load_sem.at[0]),
        pltpu.make_async_copy(codes, codes_v, load_sem.at[1]),
        pltpu.make_async_copy(scales, scales_v, load_sem.at[2]),
        pltpu.make_async_copy(queries.at[0], queries_v, load_sem.at[3]),
        pltpu.make_async_copy(base.at[0, pl.ds(g * chunk, chunk), :], base_v.at[core], load_sem.at[4]),
    ]
    for load in loads:
        load.start()
    caches = []
    for r in range(rows):
        caches.append(
            (
                pltpu.make_async_copy(keys.at[0, r, 0], keys_v.at[r], cache_sem.at[0, r]),
                pltpu.make_async_copy(values.at[0, r, 0], values_v.at[r], cache_sem.at[1, r]),
            )
        )
        for load in caches[r]:
            load.start()

    loads[0].wait()
    slab = jnp.concatenate([hidden_v[r].astype(jnp.float32) for r in range(rows)], axis=0)
    for h in range(2):
        half_out[h] = slab[:, h * chunk : (h + 1) * chunk].astype(jnp.bfloat16)

    loads[1].wait()
    loads[2].wait()
    turned = scales_v[...].astype(jnp.float32).reshape(BLOCKS * 2, owned).T
    for b in range(BLOCKS):
        code = codes_v[b].astype(jnp.float32)
        left = code[:, :128] * turned[:, 2 * b : 2 * b + 1]
        right = code[:, 128:] * turned[:, 2 * b + 1 : 2 * b + 2]
        delta_out[b] = jnp.concatenate([left, right], axis=1).astype(jnp.bfloat16)

    pl.semaphore_wait(barrier, len(inside) + 2 + 4 * lax.div(high, 2))

    @pl.when(jnp.logical_not(early))
    def _():
        which = s * core * (HIGH - 1 - high)
        og = WIDE * (HIGH - 1 - high) * (1 - s * core) + wide
        for i in range(4):
            there = at(og, s, 2 * i + core)
            pl.semaphore_signal(ready.at[which], inc=1, device_id=there, device_id_type=MESH)

    is_early = 1 - lax.div(high, 2)
    place_there = hidden_in.at[(1 - is_early) * WIDE + wide]
    relay_core = 1 - lax.rem(high, 2)
    relay_chip = lax.rem(wide + 2 * is_early * relay_core, WIDE)

    def half_copy(h, og, target, sem):
        return pltpu.make_async_remote_copy(
            src_ref=half_out.at[h],
            dst_ref=target,
            send_sem=half_send,
            recv_sem=sem,
            device_id=at(og, s, 2 * relay_chip + relay_core),
            device_id_type=MESH,
        )

    relayed = early & (chip >= 2)
    via = is_early * lax.div(chip, 2)
    which_held = via * s * (1 - high) * (HIGH - 1 - chip)
    half_to = [WIDE * ((1 - via) * chip + via * (1 - s * (1 - high)) * (HIGH - 1 - chip)) + 2 * core + h for h in range(2)]
    stays = [(og == g) & (2 * relay_chip + relay_core == t) for og in half_to]
    for h in range(2):
        for here_first, target, sem in (
            (jnp.logical_not(relayed), place_there, half_recv.at[1 - is_early]),
            (relayed, held.at[which_held], held_recv.at[which_held]),
        ):

            @pl.when(here_first & stays[h])
            def _():
                pltpu.make_async_copy(half_out.at[h], target, sem).start()

            @pl.when(here_first & jnp.logical_not(stays[h]))
            def _():
                half_copy(h, half_to[h], target, sem).start()

    for other, there in inside:
        pltpu.make_async_remote_copy(
            src_ref=delta_out.at[other],
            dst_ref=delta_in.at[lax.rem(other, 2), me],
            send_sem=delta_send,
            recv_sem=delta_recv,
            device_id=there,
            device_id_type=MESH,
        ).start()
    pltpu.make_async_copy(delta_out.at[me], delta_in.at[core, me], delta_recv).start()

    loads[4].wait()
    base_copy = pltpu.make_async_remote_copy(
        src_ref=base_v.at[core],
        dst_ref=base_v.at[core],
        send_sem=base_send,
        recv_sem=base_recv,
        device_id=at(g, s, sibling),
        device_id_type=MESH,
    )
    base_copy.start()

    loads[3].wait()
    for r in range(rows):
        block = queries_v[r].astype(jnp.float32)
        asked[pl.ds(r * asks, asks), :] = jnp.concatenate(
            [block[:, h * 128 : (h + 1) * 128] for h in range(heads)], axis=0
        ).astype(jnp.bfloat16)

    def attend(r):
        lines = pl.ds(r * asks, asks)
        caches[r][0].wait()
        score = lax.dot_general(
            asked[lines, :], keys_v[r], (((1,), (1,)), ((), ())), preferred_element_type=jnp.float32
        ) * SCALE
        place = lax.broadcasted_iota(jnp.int32, (asks, context), 1)
        score = jnp.where(place < lengths[r], score, -jnp.inf)
        peak = jnp.max(score, axis=1, keepdims=True)
        weight = jnp.exp2(score - peak)
        total = jnp.sum(weight, axis=1, keepdims=True)
        caches[r][1].wait()
        best[lines, :] = jnp.broadcast_to(peak, (asks, 128))
        norm[lines, :] = jnp.broadcast_to(total, (asks, 128))
        mix[lines, :] = jnp.dot(weight.astype(jnp.bfloat16), values_v[r], preferred_element_type=jnp.float32)

    attend(0)
    attend(1)

    early_piece = hidden_in.at[early_wide]
    late_piece = hidden_in.at[WIDE + late_wide]

    def spread_copy(piece, sem, i):
        return pltpu.make_async_remote_copy(
            src_ref=piece,
            dst_ref=piece,
            send_sem=spread_send,
            recv_sem=spread_recv.at[sem],
            device_id=at(g, s, 2 * lax.rem(chip + i, 4) + core),
            device_id_type=MESH,
        )

    def relay_copy(k, there):
        return pltpu.make_async_remote_copy(
            src_ref=held.at[k],
            dst_ref=early_piece,
            send_sem=spread_send,
            recv_sem=spread_recv.at[early_wide],
            device_id=there,
            device_id_type=MESH,
        )

    @pl.when(early)
    def _():
        pltpu.make_async_copy(early_piece, early_piece, half_recv.at[0]).wait()
        for i in turns[:3]:
            spread_copy(early_piece, early_wide, i).start()

    for k in (1, 0):
        does, og = relays[k]

        @pl.when(does)
        def _():
            pl.semaphore_wait(ready.at[k], 4)
            pltpu.make_async_copy(held.at[k], held.at[k], held_recv.at[k]).wait()
            for there in late_cores(og):
                relay_copy(k, there).start()

    attend(2)

    mine = delta_in.at[core]
    pltpu.make_async_copy(mine, mine, delta_recv).wait()
    pass_copy = pltpu.make_async_remote_copy(
        src_ref=mine,
        dst_ref=mine,
        send_sem=pass_send,
        recv_sem=pass_recv,
        device_id=at(g, s, sibling),
        device_id_type=MESH,
    )
    pass_copy.start()

    base_copy.wait_recv()
    pass_copy.wait_recv()
    tokens = rows * steps

    def send_part(c, slot, og):
        return pltpu.make_async_remote_copy(
            src_ref=part_out.at[c, slot],
            dst_ref=part_in.at[g],
            send_sem=part_send,
            recv_sem=part_recv,
            device_id=at(og, s, 2 * chip + c),
            device_id_type=MESH,
        )

    def pass_late():
        pltpu.make_async_copy(late_piece, late_piece, half_recv.at[1]).wait()
        for i in turns[:3]:
            spread_copy(late_piece, WIDE + late_wide, i).start()

    pl.when(jnp.logical_not(early))(pass_late)
    sends = []
    for phase, taken in ((0, (0, 1)), (0, (2, 3)), (1, (0, 1, 2, 3))):
        oh = (early_rows, late_rows)[phase]
        if taken == (2, 3):
            pl.when(early)(pass_late)

        for j in taken:
            taken_here = (early & (early_wide == j)) if phase == 0 else (late_wide == j)

            @pl.when(jnp.logical_not(taken_here))
            def _():
                piece = hidden_in.at[phase * WIDE + j]
                pltpu.make_async_copy(piece, piece, spread_recv.at[phase * WIDE + j]).wait()

        slots = pl.ds(phase * WIDE + taken[0], len(taken))
        features = hidden_in[slots].reshape(len(taken) * tokens, chunk)
        for c in (1, 0):
            part = jnp.dot(features, base_v[c], preferred_element_type=jnp.float32)
            part = part + jnp.dot(
                features, delta_in[c].reshape(chunk, part.shape[1]), preferred_element_type=jnp.float32
            )
            part_out[c, slots] = part.reshape(len(taken), tokens, part.shape[1]).astype(jnp.bfloat16)
            for j in taken:
                slot = phase * WIDE + j
                og = WIDE * oh + j
                sends.append((c, slot, og))
                local = (og == g) & (core == c)

                @pl.when(local)
                def _():
                    pltpu.make_async_copy(part_out.at[c, slot], part_in.at[g], part_recv).start()

                @pl.when(jnp.logical_not(local))
                def _():
                    send_part(c, slot, og).start()

    attend(3)

    line = lax.broadcasted_iota(jnp.int32, (tokens, 128), 0)
    lane = lax.broadcasted_iota(jnp.int32, (tokens, 128), 1)
    start = jnp.zeros((tokens, 128), jnp.int32)
    for r in range(rows):
        start = jnp.where(line // steps == r, lengths[r], start)
    position = (start + line % steps).astype(jnp.float32)
    frequency = jnp.exp((lane % 64).astype(jnp.float32) * (-2.0 * math.log(1000000.0) / 128))
    phase = position * frequency
    cosine[...] = jnp.cos(phase)
    turned_sine = jnp.sin(phase)
    sine[...] = jnp.where(lane < 64, -turned_sine, turned_sine)

    for h in range(2):

        @pl.when(jnp.logical_not(stays[h]))
        def _():
            half_copy(h, g, place_there, half_recv.at[0]).wait_send()

    for i in turns[:3]:
        spread_copy(late_piece, WIDE + late_wide, i).wait_send()

    @pl.when(early)
    def _():
        for i in turns[:3]:
            spread_copy(early_piece, early_wide, i).wait_send()

    for k, (does, og) in enumerate(relays):

        @pl.when(does)
        def _():
            for there in late_cores(og):
                relay_copy(k, there).wait_send()

    sent = delta_out.at[pl.ds(0, BLOCKS - 1)]
    pltpu.make_async_copy(sent, sent, delta_send).wait()
    base_copy.wait_send()
    pass_copy.wait_send()
    for c, slot, og in sends:

        @pl.when(jnp.logical_not((og == g) & (core == c)))
        def _():
            send_part(c, slot, og).wait_send()

    pltpu.make_async_copy(part_in, part_in, part_recv).wait()
    projected[...] = jnp.sum(part_in[...].astype(jnp.float32), axis=0)


def finish(projected, asked, best, norm, mix, cosine, sine, entries, attended, entries_v, attended_v, store_sem):
    rows, steps = entries_v.shape[0], entries_v.shape[1]
    tokens = rows * steps
    total = asked.shape[0]
    asks = total // rows
    heads = asks // steps

    key = projected[:, :128]
    swapped = jnp.concatenate([key[:, 64:], key[:, :64]], axis=1)
    fresh_key = key * cosine[...] + swapped * sine[...]
    fresh_value = projected[:, 128:]
    for r in range(rows):
        lines = slice(r * steps, (r + 1) * steps)
        entries_v[r] = jnp.concatenate([fresh_key[lines], fresh_value[lines]], axis=1).astype(jnp.bfloat16)
    store_entries = pltpu.make_async_copy(entries_v, entries.at[0], store_sem.at[0])
    store_entries.start()

    score = lax.dot_general(
        asked[...], fresh_key.astype(jnp.bfloat16), (((1,), (1,)), ((), ())), preferred_element_type=jnp.float32
    ) * SCALE
    line = lax.broadcasted_iota(jnp.int32, (total, tokens), 0)
    col = lax.broadcasted_iota(jnp.int32, (total, tokens), 1)
    seen = (line // asks == col // steps) & (col % steps <= line % steps)
    score = jnp.where(seen, score, -jnp.inf)
    old = best[:, :1]
    peak = jnp.maximum(old, jnp.max(score, axis=1, keepdims=True))
    weight = jnp.exp2(score - peak)
    decay = jnp.exp2(old - peak)
    whole = norm[:, :1] * decay + jnp.sum(weight, axis=1, keepdims=True)
    result = mix[...] * decay + jnp.dot(
        weight.astype(jnp.bfloat16), fresh_value.astype(jnp.bfloat16), preferred_element_type=jnp.float32
    )
    result = result / whole
    for r in range(rows):
        for h in range(heads):
            at = r * asks + h * steps
            attended_v[r, :, h * 128 : (h + 1) * 128] = result[at : at + steps].astype(jnp.bfloat16)
    store_attended = pltpu.make_async_copy(attended_v, attended.at[0], store_sem.at[1])
    store_attended.start()
    store_entries.wait()
    store_attended.wait()


def body(hidden, base_kv, delta_codes, delta_scales, queries, key_cache, value_cache, lengths):
    rows, steps, slab = hidden.shape[1:]
    owned, width = delta_codes.shape[1:]
    chunk = BLOCKS * owned
    context = key_cache.shape[3]
    query_width = queries.shape[3]
    tokens = rows * steps
    asks = rows * query_width // 128 * steps
    anywhere = pl.BlockSpec(memory_space=pl.ANY)
    scalars = pl.BlockSpec(memory_space=pltpu.SMEM)
    fast = pl.BlockSpec(memory_space=pltpu.VMEM)
    bf16, f32 = jnp.bfloat16, jnp.float32
    dma = pltpu.SemaphoreType.DMA
    middle = pl.pallas_call(
        exchange,
        out_shape=(
            pltpu.VMEM((tokens, width), f32),
            pltpu.VMEM((asks, 128), bf16),
            pltpu.VMEM((asks, 128), f32),
            pltpu.VMEM((asks, 128), f32),
            pltpu.VMEM((asks, 128), f32),
            pltpu.VMEM((tokens, 128), f32),
            pltpu.VMEM((tokens, 128), f32),
        ),
        in_specs=[anywhere] * 7 + [scalars],
        out_specs=[fast] * 7,
        scratch_shapes=[
            pltpu.VMEM((rows, steps, slab), bf16),
            pltpu.VMEM((rows, steps, query_width), bf16),
            pltpu.VMEM((BLOCKS, owned, width), bf16),
            pltpu.VMEM((BLOCKS, 2, owned), bf16),
            pltpu.VMEM((2, chunk, width), bf16),
            pltpu.VMEM((rows, context, 128), bf16),
            pltpu.VMEM((rows, context, 128), bf16),
            pltpu.VMEM((BLOCKS, owned, width), bf16),
            pltpu.VMEM((2, BLOCKS, owned, width), bf16),
            pltpu.VMEM((2, tokens, chunk), bf16),
            pltpu.VMEM((HALF, tokens, chunk), bf16),
            pltpu.VMEM((2, tokens, chunk), bf16),
            pltpu.VMEM((2, HALF, tokens, width), bf16),
            pltpu.VMEM((GROUPS, tokens, width), bf16),
            dma((5,)),
            dma((2, rows)),
            dma, dma, dma, dma, dma, dma, dma,
            dma((2,)), dma((2,)), dma, dma((2 * WIDE,)), dma, dma, pltpu.SemaphoreType.REGULAR((2,)),
        ],
        compiler_params=pltpu.CompilerParams(
            collective_id=0, has_side_effects=True, vmem_limit_bytes=60 * 1024 * 1024
        ),
    )(
        hidden, base_kv, delta_codes, jnp.transpose(delta_scales, (0, 2, 1)),
        queries, key_cache, value_cache, lengths,
    )
    return pl.pallas_call(
        finish,
        out_shape=(
            jax.ShapeDtypeStruct((1, rows, steps, width), bf16),
            jax.ShapeDtypeStruct((1, rows, steps, query_width), bf16),
        ),
        in_specs=[fast] * 7,
        out_specs=[anywhere, anywhere],
        scratch_shapes=[
            pltpu.VMEM((rows, steps, width), bf16),
            pltpu.VMEM((rows, steps, query_width), bf16),
            dma((2,)),
        ],
        compiler_params=pltpu.CompilerParams(vmem_limit_bytes=8 * 1024 * 1024),
    )(*middle)


def solution(mesh):
    placed = (
        P("section", "group", None, "tensor"),
        P(("section", "tensor"), None, None),
        P(None, ("group", "section", "tensor"), None),
        P(None, ("group", "section", "tensor"), None),
        P("section", "group", None, "tensor"),
        P("section", "group", "tensor", None, None),
        P("section", "group", "tensor", None, None),
        P("group"),
    )
    return jax.shard_map(
        body,
        mesh=mesh,
        in_specs=placed,
        out_specs=(P("section", "group", None, "tensor"), P("section", "group", None, "tensor")),
        check_vma=False,
    )
```
